256 devices in a mesh: dp: 4 (over x), expert: 64 (over z, y, core).
Axes of the slice: x: 4, y: 4, z: 8, core: 2. Of those that a mesh axis runs over, the one named last changes fastest.
Arguments:
- stream_rows: bfloat16 [32768, 2880], P(('dp', 'expert')), may hold values from -6 to 6
- query_rows: bfloat16 [32768, 2048], P(('dp', 'expert')), may hold values from -150 to 150
- key_value_rows: bfloat16 [32768, 512], P(('dp', 'expert')), may hold values from -12 to 12
- destination: int32 [32768], P(('dp', 'expert')), may hold values from 0 to 32767, as said below
- lengths: int32 [64, 3], P('expert'), may hold values from 1 to 256, 512 in all within a row
- out_weight: bfloat16 [2048, 2880], P(None, 'dp'), may hold values from -0.125 to 0.125
- expert_index: int32 [64, 512, 4], P('expert', 'dp'), may hold values from 0 to 63, all different within a row
- router_weights: float32 [64, 512, 4], P('expert', 'dp'), may hold values from 0.1 to 0.6
- gate_up: bfloat16 [64, 2880, 2880], P('expert', None, 'dp'), may hold values from -0.109375 to 0.109375
- down_weight: bfloat16 [64, 1440, 2880], P('expert', 'dp'), may hold values from -0.15625 to 0.15625
Outputs:
- scored: bfloat16 [64, 512, 2880], P('expert', 'dp')
The draws below stay inside these ranges and needn't reach their ends.
Inputs may be any that keep to these rules, and one draw needn't show every extreme that they name: destination is a permutation of the 32768 scorer rows. Generator block b of 128 rows (rows b * 128 onward, b = p * 64 + e for dp index p and expert index e) sends exactly 2 rows to every pack, all to positions p * 128 to (p + 1) * 128 - 1 of that pack.
All inputs are finite; a program needn't handle non-finite values.
Results may differ from the reference program's by a relative error of at most 0.012.
Values may be sent and summed in bfloat16 or wider, within the bound.
A program may use at most 128 MiB of HBM per device.

```python
import math
import jax
import jax.numpy as jnp
import numpy as np
from jax import lax

D = 2880
HEADS = 32
KV_HEADS = 4
HEAD_DIM = 64
FF = 1440
TOPK = 4
SEGS = 3
TOK_DEV = 128
PACKS = 64
SEQ = 512
TOKENS = 32768
EXPERTS = 64
CAP = 8
SEG_MOST = 256


def draw_query_rows(key, part):
    key = jax.random.fold_in(key, 31)
    first = jax.random.fold_in(key, 0)
    noise = jax.random.normal(first, (TOKENS, HEADS, HEAD_DIM), jnp.float32)
    values = noise
    return jnp.clip(values.reshape(TOKENS, HEADS * HEAD_DIM), -150.0, 150.0).astype(jnp.bfloat16)


def draw_key_value_rows(key, part):
    key = jax.random.fold_in(key, 32)
    first, second = jax.random.split(key)
    noise = jax.random.normal(first, (TOKENS, KV_HEADS, HEAD_DIM), jnp.float32)
    value_part = jax.random.normal(second, (TOKENS, KV_HEADS * HEAD_DIM), jnp.float32)
    key_part = noise
    joined = jnp.concatenate([key_part.reshape(TOKENS, KV_HEADS * HEAD_DIM), value_part], axis=1)
    return jnp.clip(joined, -12.0, 12.0).astype(jnp.bfloat16)


def draw_destination(key, part):
    key = jax.random.fold_in(key, 45)
    first, second = jax.random.split(key)
    dp_count = SEQ // TOK_DEV
    share = TOK_DEV // PACKS
    keys_target = jax.random.split(first, dp_count * PACKS)
    target_perm = jax.vmap(lambda single: jax.random.permutation(single, TOK_DEV))(keys_target)
    target_perm = target_perm.reshape(dp_count, PACKS, PACKS, share)
    chosen = jnp.transpose(target_perm, (0, 2, 1, 3))
    pack_ids = jnp.arange(PACKS, dtype=jnp.int32)[None, None, :, None]
    block_ids = jnp.arange(dp_count, dtype=jnp.int32)[:, None, None, None]
    flat_target = (pack_ids * SEQ + block_ids * TOK_DEV + chosen).reshape(dp_count, PACKS, TOK_DEV)
    keys_source = jax.random.split(second, dp_count * PACKS)
    source_perm = jax.vmap(lambda single: jax.random.permutation(single, TOK_DEV))(keys_source)
    source_perm = source_perm.reshape(dp_count, PACKS, TOK_DEV)
    shuffled = jnp.take_along_axis(flat_target, source_perm, axis=2)
    return shuffled.reshape(TOKENS).astype(jnp.int32)


def levels(stream_key, shape, cuts, least, high):
    level, own = 1.0, jax.random.fold_in(stream_key, 6)
    for position, shards_of in cuts:
        heights = jnp.exp(jax.random.uniform(jax.random.fold_in(own, position), (shards_of,), jnp.float32, least / len(cuts), high / len(cuts)))
        level = level * jnp.repeat(heights, shape[position] // shards_of).reshape([-1 if axis == position else 1 for axis in range(len(shape))])
    return level


def picks_of(key, rows, count, top, lift):
    ranking = jax.random.permutation(jax.random.fold_in(key, 1), count)
    boost = ranking
    for power in range(3):
        boost = boost * boost // count
    boost = boost * lift // count
    tickets = jax.random.randint(jax.random.fold_in(key, 2), (rows, count), 0, 4096) + boost
    fixed_rows = jax.random.permutation(jax.random.fold_in(key, 3), rows)[jnp.arange(count) % rows]
    tickets = jnp.where(jnp.arange(rows)[:, None] == fixed_rows[None, :], 1 << 14, tickets)
    merit = tickets * count + jnp.arange(count)
    return lax.top_k(merit.astype(jnp.int32), top)[1].astype(jnp.int32)


def split_up(amount, total, most, skew):
    loads = [(1 << 20) // math.isqrt(grade ** skew) + 1 for grade in range(2, amount + 1)]
    rest, holding = total - most - (amount - 1), [1] * (amount - 1)
    while rest > 0:
        movable = [i for i in range(amount - 1) if holding[i] < most]
        pool, budget = sum([loads[i] for i in movable]), rest
        for i in movable:
            extra = min(most - holding[i], max(1, budget * loads[i] // pool), rest)
            holding[i] = holding[i] + extra
            rest = rest - extra
    return np.array([most] + holding)


def uneven(stream_key, amount, total, reach, slope):
    if amount == 2:
        one = jax.random.randint(stream_key, (), max(1, total - reach), min(reach, total - 1) + 1)
        return jnp.stack([one, total - one])
    sizes = jnp.asarray(split_up(amount, total, reach, slope), jnp.int32)
    couples = (amount - 1) // 2
    giver, receiver = sizes[1:1 + 2 * couples:2], sizes[2:2 + 2 * couples:2]
    slack = jnp.minimum(giver - 1, reach - receiver)
    shifted = jax.random.randint(jax.random.fold_in(stream_key, 1), (couples,), 0, 1 << 20) % (slack + 1)
    sizes = sizes.at[1:1 + 2 * couples:2].set(giver - shifted).at[2:2 + 2 * couples:2].set(receiver + shifted)
    return sizes[jax.random.permutation(jax.random.fold_in(stream_key, 2), amount)]


def bell_draw(stream_key, extent, width, bound, cuts=(), kind=jnp.bfloat16):
    array = width * jax.random.normal(stream_key, extent, jnp.float32)
    if cuts:
        array = array * levels(stream_key, extent, cuts, -0.22, 0.18)
    return jnp.clip(array, -bound, bound).astype(kind)


def setup_inputs(seed: int = 0) -> dict:
    key_list = jax.random.split(jax.random.key(seed), 11)
    stream_rows = bell_draw(key_list[0], (TOKENS, D), 1.0, 6.0, ((0, 256),))
    query_rows = draw_query_rows(jax.random.fold_in(key_list[10], 71), 0)
    key_value_rows = draw_key_value_rows(jax.random.fold_in(key_list[10], 71), 0)
    destination = draw_destination(jax.random.fold_in(key_list[10], 71), 0)
    lengths = jax.vmap(lambda own: uneven(own, SEGS, SEQ, SEG_MOST, 1))(jax.random.split(key_list[4], PACKS)).reshape((PACKS, SEGS)).astype(jnp.int32)
    out_weight = bell_draw(key_list[5], (HEADS * HEAD_DIM, D), (HEADS * HEAD_DIM) ** -0.5, 0.125, ((1, 4),))
    expert_index = picks_of(key_list[6], PACKS * SEQ, EXPERTS, TOPK, 512).reshape((PACKS, SEQ, TOPK))
    router_weights = jnp.clip(0.1 + 0.5 * jax.random.uniform(key_list[7], (PACKS, SEQ, TOPK), jnp.float32) ** levels(key_list[7], (PACKS, SEQ, TOPK), ((0, 64), (1, 4)), -0.2, 0.2), 0.1, 0.6)
    gate_up = bell_draw(key_list[8], (EXPERTS, D, 2 * FF), D ** -0.5, 0.109375, ((0, 64), (2, 4)))
    down_weight = bell_draw(key_list[9], (EXPERTS, FF, D), FF ** -0.5, 0.15625, ((0, 64), (1, 4)))
    return {"stream_rows": stream_rows, "query_rows": query_rows, "key_value_rows": key_value_rows, "destination": destination, "lengths": lengths, "out_weight": out_weight, "expert_index": expert_index, "router_weights": router_weights, "gate_up": gate_up, "down_weight": down_weight}


def reorder_rows(rows, destination):
    return jnp.zeros_like(rows).at[destination].set(rows)

def segment_number(seg_ends, positions):
    return lax.optimization_barrier(jnp.sum((positions[:, None] >= seg_ends[None, :]).astype(jnp.int32), axis=1)).astype(jnp.int32)

def gated_units(projected):
    gate_part = projected[:, 0::2]
    up_part = projected[:, 1::2]
    return ((up_part + 1.0) * gate_part * jax.nn.sigmoid(1.702 * gate_part)).astype(jnp.bfloat16)

def attend_pack(inputs):
    queries, memory, pack_lengths = inputs
    group_size = HEADS // KV_HEADS
    key_width = KV_HEADS * HEAD_DIM
    positions = jnp.arange(SEQ, dtype=jnp.int32)
    seg_ends = jnp.cumsum(pack_lengths)[:-1].astype(jnp.int32)
    segment = segment_number(seg_ends, positions)
    visible = (segment[:, None] == segment[None, :]) & (positions[None, :] <= positions[:, None])
    query_heads = queries.reshape(SEQ, KV_HEADS, group_size, HEAD_DIM).astype(jnp.float32)
    key_block = memory[:, :key_width].reshape(SEQ, KV_HEADS, HEAD_DIM).astype(jnp.float32)
    value_block = memory[:, key_width:].reshape(SEQ, KV_HEADS, HEAD_DIM).astype(jnp.float32)
    scores = jnp.einsum('tkgd,nkd->kgtn', query_heads, key_block, precision=lax.Precision.HIGHEST) * HEAD_DIM ** (-0.5)
    scores = jnp.where(visible, scores, -1e+30)
    row_max = lax.optimization_barrier(jnp.max(scores, axis=-1, keepdims=True))
    weights = jnp.where(visible, jnp.exp(scores - row_max), 0.0)
    denominator = lax.optimization_barrier(jnp.sum(weights, axis=-1))
    rounded = lax.optimization_barrier(weights.astype(jnp.bfloat16)).astype(jnp.float32)
    numerator = jnp.einsum('kgtn,nkd->kgtd', rounded, value_block, precision=lax.Precision.HIGHEST)
    context = numerator / denominator[..., None]
    return context.transpose(2, 0, 1, 3).reshape(SEQ, HEADS * HEAD_DIM).astype(jnp.bfloat16)

def reference(stream_rows, query_rows, key_value_rows, destination, lengths, out_weight, expert_index, router_weights, gate_up, down_weight):
    stream = reorder_rows(stream_rows, destination)
    queries = reorder_rows(query_rows, destination)
    memory = reorder_rows(key_value_rows, destination)
    context = lax.map(attend_pack, (queries.reshape(PACKS, SEQ, HEADS * HEAD_DIM), memory.reshape(PACKS, SEQ, 2 * KV_HEADS * HEAD_DIM), lengths))
    context = context.reshape(TOKENS, HEADS * HEAD_DIM)
    residual = stream.astype(jnp.float32) + jnp.dot(context, out_weight, preferred_element_type=jnp.float32)
    normed = (residual * lax.rsqrt(lax.optimization_barrier(jnp.mean(residual * residual, axis=-1, keepdims=True)) + 1e-05)).astype(jnp.bfloat16)
    block_count = TOKENS // TOK_DEV
    entry_count = TOK_DEV * TOPK
    flat_index = expert_index.reshape(block_count, entry_count).astype(jnp.int32)
    onehot = (flat_index[:, :, None] == jnp.arange(EXPERTS, dtype=jnp.int32)[None, None, :]).astype(jnp.int32)
    slot_index = lax.optimization_barrier(jnp.sum(onehot * (jnp.cumsum(onehot, axis=1) - 1), axis=2)).astype(jnp.int32)
    kept_mask = slot_index < CAP
    safe_slot = jnp.where(kept_mask, slot_index, CAP).astype(jnp.int32)
    block_ids = jnp.broadcast_to(jnp.arange(block_count, dtype=jnp.int32)[:, None], (block_count, entry_count))
    source_row = (block_ids * TOK_DEV + jnp.arange(entry_count, dtype=jnp.int32)[None, :] // TOPK).astype(jnp.int32)
    table = jnp.full((EXPERTS, block_count, CAP), TOKENS, jnp.int32).at[flat_index, block_ids, safe_slot].set(source_row, mode='drop')
    slot_weight = jnp.zeros((EXPERTS, block_count, CAP), jnp.float32).at[flat_index, block_ids, safe_slot].set(router_weights.reshape(block_count, entry_count), mode='drop')
    padded = jnp.concatenate([normed, jnp.zeros((1, D), jnp.bfloat16)], axis=0)

    def expert_step(mixture, items):
        rows_index, weight_table, local_in, local_out = items
        flat_rows = rows_index.reshape(-1)
        token_rows = padded[flat_rows]
        hidden = gated_units(jnp.dot(token_rows, local_in, preferred_element_type=jnp.float32))
        expert_out = jnp.dot(hidden, local_out, preferred_element_type=jnp.float32).astype(jnp.bfloat16)
        term = lax.optimization_barrier(expert_out).astype(jnp.float32) * weight_table.reshape(-1, 1)
        return (mixture.at[flat_rows].add(term, mode='drop'), None)
    mixture, unused = lax.scan(expert_step, jnp.zeros((TOKENS, D), jnp.float32), (table, slot_weight, gate_up, down_weight))
    return (residual + mixture).astype(jnp.bfloat16).reshape(PACKS, SEQ, D)
```

```python
import jax
import jax.numpy as jnp
from jax import lax
from jax.sharding import PartitionSpec as P

HEADS = 32
KV_HEADS = 4
HEAD_DIM = 64
TOPK = 4


masked_score = -1e30
norm_eps = 1e-05
f32 = jnp.float32
bf16 = jnp.bfloat16


def segment_number(seg_ends, positions):
    return jnp.sum((positions[:, None] >= seg_ends[None, :]).astype(jnp.int32), axis=1)


def pick(matrix, rows):
    return jnp.dot(matrix, rows, preferred_element_type=f32).astype(bf16)


def ring_perms(dp_count, expert_count):
    turns = []
    for sign in (1, -1):
        turns.append(
            [
                (x * expert_count + e, ((x + (sign if e % 2 == 0 else -sign)) % dp_count) * expert_count + e)
                for x in range(dp_count)
                for e in range(expert_count)
            ]
        )
    return turns


def on_device(
    stream_rows,
    query_rows,
    key_value_rows,
    destination,
    lengths,
    out_weight,
    expert_index,
    router_weights,
    gate_up,
    down_weight,
):
    row_count, model_width = stream_rows.shape
    dp_count = lax.axis_size("dp")
    expert_count = lax.axis_size("expert")
    seq_len = row_count * dp_count
    my_block = lax.axis_index("dp")
    both = ("dp", "expert")
    turn, back = ring_perms(dp_count, expert_count)

    columns = gate_up.shape[2]
    units = columns // 2
    unit = jnp.arange(units, dtype=jnp.int32)
    column = jnp.arange(columns, dtype=jnp.int32)
    split = (column[None, None, :] == 2 * unit[None, :, None] + jnp.arange(2, dtype=jnp.int32)[:, None, None]).astype(bf16)
    local_in = jnp.einsum("suc,dc->sud", split, gate_up[0], preferred_element_type=f32).astype(bf16)
    local_out = down_weight[0]
    in_1 = lax.ppermute(local_in, both, turn)
    in_2 = lax.ppermute(local_in, both, back)
    out_1 = lax.ppermute(local_out, both, turn)
    out_2 = lax.ppermute(local_out, both, back)

    share = row_count // expert_count
    row_id = jnp.arange(row_count, dtype=jnp.int32)
    pack = destination // seq_len
    rank = jnp.sum(
        ((pack[:, None] == pack[None, :]) & (row_id[None, :] < row_id[:, None])).astype(jnp.int32), axis=1
    )
    send_slot = pack * share + rank
    sender = (row_id[:, None] == send_slot[None, :]).astype(bf16)
    place = jnp.broadcast_to((destination % row_count).astype(bf16)[:, None], (row_count, 128))
    attention_rows = jnp.concatenate([query_rows, key_value_rows, place], axis=1)
    query_width = query_rows.shape[1]
    memory_width = key_value_rows.shape[1]

    def exchange(rows):
        width = rows.shape[1]
        moved = lax.all_to_all(
            pick(sender, rows).reshape(expert_count, share, width),
            "expert",
            split_axis=0,
            concat_axis=0,
            tiled=True,
        )
        return moved.reshape(row_count, width)

    got = exchange(attention_rows)
    got_stream = exchange(stream_rows)
    place_got = got[:, query_width + memory_width].astype(jnp.int32)
    settle = (row_id[:, None] == place_got[None, :]).astype(bf16)
    memory = pick(settle, got[:, query_width : query_width + memory_width])
    queries = pick(settle, got[:, :query_width])
    stream = jnp.dot(settle, got_stream, preferred_element_type=f32)

    group_size = HEADS // KV_HEADS
    key_width = KV_HEADS * HEAD_DIM
    seg_ends = jnp.cumsum(lengths[0])[:-1]
    query_position = my_block * row_count + row_id
    query_segment = segment_number(seg_ends, query_position)
    query_heads = queries.reshape(row_count, KV_HEADS, group_size, HEAD_DIM)

    def shift(value, step):
        if step == 0:
            return value
        return lax.ppermute(value, "dp", [(x, (x + step) % dp_count) for x in range(dp_count)])

    section = jnp.concatenate([shift(memory, s) for s in range(dp_count)], axis=0)
    key_position = jnp.concatenate(
        [lax.rem(my_block - s + dp_count, dp_count) * row_count + row_id for s in range(dp_count)]
    )
    key_count = section.shape[0]
    key_segment = segment_number(seg_ends, key_position)
    visible = (query_segment[:, None] == key_segment[None, :]) & (
        key_position[None, :] <= query_position[:, None]
    )
    key_block = section[:, :key_width].reshape(key_count, KV_HEADS, HEAD_DIM)
    value_block = section[:, key_width:].reshape(key_count, KV_HEADS, HEAD_DIM)
    scores = jnp.einsum(
        "tkgd,nkd->kgtn", query_heads, key_block, preferred_element_type=f32
    ) * HEAD_DIM ** (-0.5)
    scores = jnp.where(visible, scores, masked_score)
    row_max = jnp.max(scores, axis=-1)
    weights = jnp.where(visible, jnp.exp(scores - row_max[..., None]), 0.0)
    denominator = jnp.sum(weights, axis=-1)
    numerator = jnp.einsum(
        "kgtn,nkd->kgtd", weights.astype(bf16), value_block, preferred_element_type=f32
    )
    context = (
        (numerator / denominator[..., None])
        .transpose(2, 0, 1, 3)
        .reshape(row_count, HEADS * HEAD_DIM)
        .astype(bf16)
    )
    parts = []
    for s in range(dp_count):
        part = jnp.dot(shift(context, s), out_weight, preferred_element_type=f32).astype(bf16)
        parts.append(shift(part, (dp_count - s) % dp_count))
    order = lax.rem(jnp.arange(dp_count, dtype=jnp.int32) - my_block + dp_count, dp_count)
    update = jnp.stack(parts)[order].transpose(1, 0, 2).reshape(row_count, model_width)
    residual = stream + update.astype(f32)
    normed = (
        residual * lax.rsqrt(jnp.mean(residual * residual, axis=-1, keepdims=True) + norm_eps)
    ).astype(bf16)

    entry_count = row_count * TOPK
    capacity = entry_count // expert_count
    flat_index = expert_index.reshape(entry_count)
    onehot = (flat_index[:, None] == jnp.arange(expert_count, dtype=jnp.int32)[None, :]).astype(
        jnp.int32
    )
    slot_index = jnp.sum(onehot * (jnp.cumsum(onehot, axis=0) - 1), axis=1)
    kept_mask = slot_index < capacity
    slots = expert_count * capacity
    target = jnp.where(kept_mask, flat_index * capacity + slot_index, slots).reshape(row_count, TOPK)
    slot_id = jnp.arange(slots, dtype=jnp.int32)
    dispatch = jnp.zeros((slots, row_count), f32)
    combine = jnp.zeros((row_count, slots), f32)
    entry_weight = router_weights.reshape(row_count, TOPK)
    for k in range(TOPK):
        dispatch = dispatch + (slot_id[:, None] == target[None, :, k]).astype(f32)
        combine = combine + jnp.where(target[:, k, None] == slot_id[None, :], entry_weight[:, k, None], 0.0)
    normed, in_1, in_2, out_1, out_2 = lax.optimization_barrier((normed, in_1, in_2, out_1, out_2))
    in_3 = lax.ppermute(in_1, both, turn)
    out_3 = lax.ppermute(out_2, both, back)
    shards = ((local_in, local_out), (in_1, out_1), (in_2, out_2), (in_3, out_3))
    outgoing = pick(dispatch.astype(bf16), normed).reshape(expert_count, capacity, model_width)
    arrived = lax.all_to_all(outgoing, "expert", split_axis=0, concat_axis=0, tiled=True)
    token_rows = arrived.reshape(-1, model_width)

    total = None
    for part_in, part_out in shards:
        gate_part = lax.dot_general(
            token_rows, part_in[0], (((1,), (1,)), ((), ())), preferred_element_type=f32
        )
        up_part = lax.dot_general(
            token_rows, part_in[1], (((1,), (1,)), ((), ())), preferred_element_type=f32
        )
        hidden = ((up_part + 1.0) * gate_part * jax.nn.sigmoid(1.702 * gate_part)).astype(bf16)
        term = jnp.dot(hidden, part_out, preferred_element_type=f32)
        total = term if total is None else total + term
    expert_out = total.astype(bf16)
    returned = lax.all_to_all(
        expert_out.reshape(arrived.shape), "expert", split_axis=0, concat_axis=0, tiled=True
    )
    flat_return = returned.reshape(slots, model_width)
    high = lax.reduce_precision(combine, 8, 7)
    low = (combine - high).astype(bf16)
    mixture = jnp.dot(high.astype(bf16), flat_return, preferred_element_type=f32) + jnp.dot(
        low, flat_return, preferred_element_type=f32
    )
    return (residual + mixture).astype(bf16).reshape(1, row_count, model_width)


def solution(mesh):
    placed = (
        P(("dp", "expert"), None),
        P(("dp", "expert"), None),
        P(("dp", "expert"), None),
        P(("dp", "expert")),
        P("expert", None),
        P(None, "dp"),
        P("expert", "dp", None),
        P("expert", "dp", None),
        P("expert", None, "dp"),
        P("expert", "dp", None),
    )
    return jax.shard_map(
        on_device, mesh=mesh, in_specs=placed, out_specs=P("expert", "dp", None), check_vma=False
    )
```

```python
import functools

import jax
import jax.numpy as jnp
from jax import lax
from jax.experimental import pallas as pl
from jax.experimental.pallas import tpu as pltpu
from jax.sharding import PartitionSpec as P

HEADS = 32
KV_HEADS = 4
HEAD_DIM = 64
TOPK = 4


masked_score = -1e30
norm_eps = 1e-05
f32 = jnp.float32
bf16 = jnp.bfloat16


def segment_number(seg_ends, positions):
    return jnp.sum((positions[:, None] >= seg_ends[None, :]).astype(jnp.int32), axis=1)


def pick(matrix, rows):
    return jnp.dot(matrix, rows, preferred_element_type=f32).astype(bf16)


def relation(index, cores, ys, zs):
    per = zs * cores
    chunk, rest = index // per, index % per
    dz = rest // cores
    return dz, (chunk + zs * ys - dz) % ys, rest % cores


def peer(expert, index, sign, cores, ys, zs):
    dz, dy, dc = relation(index, cores, ys, zs)
    z, y, c = expert // (ys * cores), (expert // cores) % ys, expert % cores
    z = (z + sign * dz + zs) % zs
    y = (y + sign * dy + ys) % ys
    c = (c + dc) % cores
    return (z * ys + y) * cores + c


def expert_kernel(
    grid,
    sent,
    dispatch,
    normed,
    residual,
    combine,
    own_in,
    near_in,
    own_out,
    result,
    raw_in,
    split_in,
    raw_out,
    out_buf,
    in_own,
    in_twin,
    x_buf,
    h_buf,
    own_part,
    part_send,
    part_recv,
    ret_recv,
    local_sem,
    weight_send,
    weight_recv,
    go_send,
    go_recv,
    twin_send,
    twin_recv,
    part_ssem,
    part_rsem,
    ret_send,
    ret_rsem,
):
    cores, ys, zs = grid
    x = lax.axis_index("dp")
    e = lax.axis_index("expert")
    odd = x % 2
    pair = (x + 1 - 2 * odd, e)
    twin = ((x + 2 * odd + 3) % 4, e)
    slabs, capacity, width = out_buf.shape
    per = slabs // 4
    rows = per * capacity
    columns = raw_in.shape[1]
    units = columns // 2
    padded = split_in.shape[1] // 2
    rest = columns - sent

    def remote(src, dst, ssem, rsem, device):
        return pltpu.make_async_remote_copy(
            src_ref=src, dst_ref=dst, send_sem=ssem, recv_sem=rsem, device_id=device, device_id_type=pl.DeviceIdType.MESH
        )

    weight_in = remote(
        own_in.at[pl.ds(sent, rest)], raw_in.at[1, pl.ds(sent, rest)], weight_send.at[0], weight_recv.at[0], pair
    )
    weight_out = remote(own_out, raw_out.at[1], weight_send.at[1], weight_recv.at[1], pair)
    weight_in.start()
    weight_out.start()
    load_own = pltpu.make_async_copy(own_in, raw_in.at[0], local_sem.at[0])
    load_near = pltpu.make_async_copy(near_in, raw_in.at[1, pl.ds(0, sent)], local_sem.at[1])
    load_out = pltpu.make_async_copy(own_out, raw_out.at[0], local_sem.at[2])
    load_own.start()
    load_near.start()
    load_out.start()

    def chunk_of(ref, c):
        return ref.at[pl.ds(c * per, per)]

    def send_dispatch(c, carry):
        picked = jnp.dot(dispatch[pl.ds(c * rows, rows), :], normed[...], preferred_element_type=f32)
        out_buf[pl.ds(c * per, per)] = picked.astype(bf16).reshape(per, capacity, width)

        def one(m, carry):
            index = c * per + m
            remote(
                out_buf.at[index], in_own.at[index], go_send.at[c], go_recv.at[c], (x, peer(e, index, 1, cores, ys, zs))
            ).start()
            return carry

        lax.fori_loop(jnp.where(c == 0, 1, 0), per, one, 0)
        return carry

    lax.fori_loop(0, 4, send_dispatch, 0)
    in_own[0] = out_buf[0]

    row = lax.broadcasted_iota(jnp.int32, (2 * padded, columns), 0)
    column = lax.broadcasted_iota(jnp.int32, (2 * padded, columns), 1)
    unit = jnp.where(row < padded, row, row - padded)
    wanted = jnp.where(unit < units, 2 * unit + jnp.where(row < padded, 0, 1), -1)
    part = (column == wanted).astype(f32).astype(bf16)

    def separate(k):
        for start in range(0, width, 768):
            cols = pl.ds(start, min(768, width - start))
            split_in[k, :, cols] = jnp.dot(part, raw_in[k, :, cols], preferred_element_type=f32).astype(bf16)

    load_own.wait()
    separate(0)

    def lead(ref, c):
        return ref.at[pl.ds(c * per, per)]

    def wait_own(c):
        @pl.when(c == 0)
        def _():
            view = in_own.at[pl.ds(1, per - 1)]
            remote(view, view, go_send.at[0], go_recv.at[0], twin).wait_recv()

        @pl.when(c > 0)
        def _():
            view = chunk_of(in_own, c)
            remote(view, view, go_send.at[c], go_recv.at[c], twin).wait_recv()

    def forward(c):
        return remote(chunk_of(in_own, c), chunk_of(in_twin, c), twin_send.at[c], twin_recv.at[c], twin)

    def partial(c):
        return remote(chunk_of(part_send, c), chunk_of(part_recv, c), part_ssem.at[c], part_rsem.at[c], twin)

    def wait_sent(ref, sems, c):
        @pl.when(c == 0)
        def _():
            view = ref.at[pl.ds(1, per - 1)]
            remote(view, view, sems.at[0], go_recv.at[0], twin).wait_send()

        @pl.when(c > 0)
        def _():
            view = chunk_of(ref, c)
            remote(view, view, sems.at[c], go_recv.at[c], twin).wait_send()

    def compute(c):
        x_buf[pl.ds(0, rows), :] = in_own[pl.ds(c * per, per)].reshape(rows, width)
        x_buf[pl.ds(rows, rows), :] = in_twin[pl.ds(c * per, per)].reshape(rows, width)

        def units_of(k, carry):
            projected = lax.dot_general(
                x_buf[...], split_in[k], (((1,), (1,)), ((), ())), preferred_element_type=f32
            )
            gate = projected[:, :padded]
            up = projected[:, padded:]
            hidden = (up + 1.0) * gate * (1.0 / (1.0 + jnp.exp(-1.702 * gate)))
            h_buf[k] = hidden.astype(bf16)
            return carry

        lax.fori_loop(0, 2, units_of, 0)
        for start in range(0, width, 768):
            size = min(768, width - start)
            cols = pl.ds(start, size)
            total = jnp.dot(h_buf[0, :, :units], raw_out[0, :, cols], preferred_element_type=f32)
            total += jnp.dot(h_buf[1, :, :units], raw_out[1, :, cols], preferred_element_type=f32)
            own_part[c, :, cols] = total[:rows]
            part_send[pl.ds(c * per, per), :, cols] = total[rows:].astype(bf16).reshape(per, capacity, size)

    def give_back(c):
        wait_sent(out_buf, go_send, c)
        total = own_part[c] + part_recv[pl.ds(c * per, per)].astype(f32).reshape(rows, width)
        out_buf[pl.ds(c * per, per)] = total.astype(bf16).reshape(per, capacity, width)

        def one(m, carry):
            index = c * per + m
            remote(
                out_buf.at[index], ret_recv.at[index], ret_send.at[c], ret_rsem.at[c], (x, peer(e, index, -1, cores, ys, zs))
            ).start()
            return carry

        lax.fori_loop(jnp.where(c == 0, 1, 0), per, one, 0)

    def step(t, carry):
        @pl.when(t < 4)
        def _():
            wait_own(t)
            forward(t).start()

        @pl.when(t == 1)
        def _():
            load_near.wait()
            load_out.wait()
            weight_in.wait()
            separate(1)
            weight_out.wait()

        @pl.when((t >= 1) & (t < 5))
        def _():
            forward(t - 1).wait_recv()
            compute(t - 1)
            partial(t - 1).start()

        @pl.when(t >= 2)
        def _():
            partial(t - 2).wait_recv()
            give_back(t - 2)

        return carry

    lax.fori_loop(0, 6, step, 0)
    ret_recv[0] = out_buf[0]

    def finish(c, carry):
        forward(c).wait_send()
        partial(c).wait_send()
        wait_sent(out_buf, ret_send, c)

        @pl.when(c == 0)
        def _():
            view = ret_recv.at[pl.ds(1, per - 1)]
            remote(view, view, go_send.at[0], ret_rsem.at[0], twin).wait_recv()

        @pl.when(c > 0)
        def _():
            view = chunk_of(ret_recv, c)
            remote(view, view, go_send.at[0], ret_rsem.at[c], twin).wait_recv()

        return carry

    lax.fori_loop(0, 4, finish, 0)
    for start in range(0, width, 768):
        size = min(768, width - start)
        cols = pl.ds(start, size)
        back = ret_recv[:, :, cols].reshape(slabs * capacity, size)
        mixed = jnp.dot(combine[0], back, preferred_element_type=f32)
        mixed += jnp.dot(combine[1], back, preferred_element_type=f32)
        result[:, cols] = (residual[:, cols] + mixed).astype(bf16)


def experts(grid, sent, dispatch, normed, residual, combine, own_in, near_in, own_out):
    slots, row_count = dispatch.shape
    width = normed.shape[1]
    columns = own_in.shape[0]
    units = columns // 2
    padded = -(-units // 128) * 128
    slabs = grid[0] * grid[1] * grid[2]
    capacity = slots // slabs
    rows = slots // 4
    vmem = pl.BlockSpec(memory_space=pltpu.VMEM)
    hbm = pl.BlockSpec(memory_space=pl.ANY)
    dma = pltpu.SemaphoreType.DMA
    buffer = pltpu.VMEM((slabs, capacity, width), bf16)
    return pl.pallas_call(
        functools.partial(expert_kernel, grid, sent),
        out_shape=jax.ShapeDtypeStruct((row_count, width), bf16),
        in_specs=[vmem, vmem, vmem, vmem, hbm, hbm, hbm],
        out_specs=vmem,
        scratch_shapes=[
            pltpu.VMEM((2, columns, width), bf16),
            pltpu.VMEM((2, 2 * padded, width), bf16),
            pltpu.VMEM((2, units, width), bf16),
            buffer,
            buffer,
            buffer,
            pltpu.VMEM((2 * rows, width), bf16),
            pltpu.VMEM((2, 2 * rows, padded), bf16),
            pltpu.VMEM((4, rows, width), f32),
            buffer,
            buffer,
            buffer,
            dma((3,)),
            dma((2,)),
            dma((2,)),
        ]
        + [dma((4,))] * 8,
        compiler_params=pltpu.CompilerParams(has_side_effects=True, vmem_limit_bytes=60 << 20),
        cost_estimate=pl.CostEstimate(flops=14 << 30, bytes_accessed=30 << 20, transcendentals=0),
        name="experts",
    )(dispatch, normed, residual, combine, own_in, near_in, own_out)


def on_device(
    stream_rows,
    query_rows,
    key_value_rows,
    destination,
    lengths,
    out_weight,
    expert_index,
    router_weights,
    gate_up,
    down_weight,
):
    row_count, model_width = stream_rows.shape
    dp_count = lax.axis_size("dp")
    expert_count = lax.axis_size("expert")
    seq_len = row_count * dp_count
    my_block = lax.axis_index("dp")
    both = ("dp", "expert")
    cores, ys = 2, 4
    grid = (cores, ys, expert_count // (cores * ys))
    own_in = gate_up[0].T
    own_out = down_weight[0]
    sent = own_in.shape[0] // 32 * 16
    near_in = lax.ppermute(own_in[:sent], "dp", [(d, d + 1 - 2 * (d % 2)) for d in range(dp_count)])

    share = row_count // expert_count
    row_id = jnp.arange(row_count, dtype=jnp.int32)
    pack = destination // seq_len
    rank = jnp.sum(
        ((pack[:, None] == pack[None, :]) & (row_id[None, :] < row_id[:, None])).astype(jnp.int32), axis=1
    )
    send_slot = pack * share + rank
    sender = (row_id[:, None] == send_slot[None, :]).astype(bf16)
    place = jnp.broadcast_to((destination % row_count).astype(bf16)[:, None], (row_count, 128))
    attention_rows = jnp.concatenate([query_rows, key_value_rows, place], axis=1)
    query_width = query_rows.shape[1]
    memory_width = key_value_rows.shape[1]

    def exchange(rows):
        width = rows.shape[1]
        moved = lax.all_to_all(
            pick(sender, rows).reshape(expert_count, share, width),
            "expert",
            split_axis=0,
            concat_axis=0,
            tiled=True,
        )
        return moved.reshape(row_count, width)

    got = exchange(attention_rows)
    got_stream = exchange(stream_rows)
    place_got = got[:, query_width + memory_width].astype(jnp.int32)
    settle = (row_id[:, None] == place_got[None, :]).astype(bf16)
    memory = pick(settle, got[:, query_width : query_width + memory_width])
    queries = pick(settle, got[:, :query_width])
    stream = jnp.dot(settle, got_stream, preferred_element_type=f32)

    group_size = HEADS // KV_HEADS
    key_width = KV_HEADS * HEAD_DIM
    seg_ends = jnp.cumsum(lengths[0])[:-1]
    query_position = my_block * row_count + row_id
    query_segment = segment_number(seg_ends, query_position)
    query_heads = queries.reshape(row_count, KV_HEADS, group_size, HEAD_DIM)

    def shift(value, step):
        if step == 0:
            return value
        return lax.ppermute(value, "dp", [(x, (x + step) % dp_count) for x in range(dp_count)])

    section = jnp.concatenate([shift(memory, s) for s in range(dp_count)], axis=0)
    key_position = jnp.concatenate(
        [lax.rem(my_block - s + dp_count, dp_count) * row_count + row_id for s in range(dp_count)]
    )
    key_count = section.shape[0]
    key_segment = segment_number(seg_ends, key_position)
    visible = (query_segment[:, None] == key_segment[None, :]) & (
        key_position[None, :] <= query_position[:, None]
    )
    key_block = section[:, :key_width].reshape(key_count, KV_HEADS, HEAD_DIM)
    value_block = section[:, key_width:].reshape(key_count, KV_HEADS, HEAD_DIM)
    scores = jnp.einsum(
        "tkgd,nkd->kgtn", query_heads, key_block, preferred_element_type=f32
    ) * HEAD_DIM ** (-0.5)
    scores = jnp.where(visible, scores, masked_score)
    row_max = jnp.max(scores, axis=-1)
    weights = jnp.where(visible, jnp.exp(scores - row_max[..., None]), 0.0)
    denominator = jnp.sum(weights, axis=-1)
    numerator = jnp.einsum(
        "kgtn,nkd->kgtd", weights.astype(bf16), value_block, preferred_element_type=f32
    )
    context = (
        (numerator / denominator[..., None])
        .transpose(2, 0, 1, 3)
        .reshape(row_count, HEADS * HEAD_DIM)
        .astype(bf16)
    )
    parts = []
    for s in range(dp_count):
        part = jnp.dot(shift(context, s), out_weight, preferred_element_type=f32).astype(bf16)
        parts.append(shift(part, (dp_count - s) % dp_count))
    order = lax.rem(jnp.arange(dp_count, dtype=jnp.int32) - my_block + dp_count, dp_count)
    update = jnp.stack(parts)[order].transpose(1, 0, 2).reshape(row_count, model_width)
    residual = stream + update.astype(f32)
    normed = (
        residual * lax.rsqrt(jnp.mean(residual * residual, axis=-1, keepdims=True) + norm_eps)
    ).astype(bf16)

    entry_count = row_count * TOPK
    capacity = entry_count // expert_count
    flat_index = expert_index.reshape(entry_count)
    onehot = (flat_index[:, None] == jnp.arange(expert_count, dtype=jnp.int32)[None, :]).astype(
        jnp.int32
    )
    slot_index = jnp.sum(onehot * (jnp.cumsum(onehot, axis=0) - 1), axis=1)
    kept_mask = slot_index < capacity
    slots = expert_count * capacity
    slab = jnp.arange(expert_count, dtype=jnp.int32)
    holder = peer(lax.axis_index("expert"), slab, 1, *grid)
    slab_expert = jnp.repeat(holder, capacity)
    slab_slot = jnp.tile(jnp.arange(capacity, dtype=jnp.int32), expert_count)
    slot_id = slab_expert * capacity + slab_slot
    target = jnp.where(kept_mask, flat_index * capacity + slot_index, slots).reshape(row_count, TOPK)
    dispatch = jnp.zeros((slots, row_count), f32)
    combine = jnp.zeros((row_count, slots), f32)
    entry_weight = router_weights.reshape(row_count, TOPK)
    for k in range(TOPK):
        dispatch = dispatch + (slot_id[:, None] == target[None, :, k]).astype(f32)
        combine = combine + jnp.where(target[:, k, None] == slot_id[None, :], entry_weight[:, k, None], 0.0)
    high = lax.reduce_precision(combine, 8, 7)
    low = (combine - high).astype(bf16)
    combine = jnp.stack([high.astype(bf16), low])
    scored = experts(grid, sent, dispatch.astype(bf16), normed, residual, combine, own_in, near_in, own_out)
    return scored.reshape(1, row_count, model_width)


def solution(mesh):
    placed = (
        P(("dp", "expert"), None),
        P(("dp", "expert"), None),
        P(("dp", "expert"), None),
        P(("dp", "expert")),
        P("expert", None),
        P(None, "dp"),
        P("expert", "dp", None),
        P("expert", "dp", None),
        P("expert", None, "dp"),
        P("expert", "dp", None),
    )
    return jax.shard_map(
        on_device, mesh=mesh, in_specs=placed, out_specs=P("expert", "dp", None), check_vma=False
    )
```

```python
import functools

import jax
import jax.numpy as jnp
from jax import lax
from jax.experimental import pallas as pl
from jax.experimental.pallas import tpu as pltpu
from jax.sharding import PartitionSpec as P

HEADS = 32
KV_HEADS = 4
HEAD_DIM = 64
TOPK = 4


masked_score = -1e30
norm_eps = 1e-05
f32 = jnp.float32
bf16 = jnp.bfloat16


def segment_number(seg_ends, positions):
    return jnp.sum((positions[:, None] >= seg_ends[None, :]).astype(jnp.int32), axis=1)


def pick(matrix, rows):
    return jnp.dot(matrix, rows, preferred_element_type=f32).astype(bf16)


def relation(index, cores, ys, zs):
    per = zs * cores
    half = max(zs // 2, 1)
    chunk, rest = index // per, index % per
    turn = rest // cores
    dz = (turn % 2) * (half + turn // 2) + (1 - turn % 2) * ((half - turn // 2) % half)
    return dz, (chunk + zs * ys - dz) % ys, rest % cores


def peer(expert, index, sign, cores, ys, zs):
    dz, dy, dc = relation(index, cores, ys, zs)
    z, y, c = expert // (ys * cores), (expert // cores) % ys, expert % cores
    z = (z + sign * dz + zs) % zs
    y = (y + sign * dy + ys) % ys
    c = (c + dc) % cores
    return (z * ys + y) * cores + c


def weight_pair(x, core):
    return (x + 5 - 2 * ((x + core) % 2)) % 4


def expert_kernel(
    grid,
    dispatch,
    normed,
    residual,
    combine,
    own_in,
    near_in,
    own_out,
    result,
    raw_in,
    split_in,
    raw_out,
    out_buf,
    in_own,
    in_twin,
    x_buf,
    h_buf,
    own_part,
    part_send,
    part_recv,
    ret_recv,
    local_sem,
    weight_send,
    weight_recv,
    go_send,
    go_recv,
    twin_send,
    twin_recv,
    part_ssem,
    part_rsem,
    ret_send,
    ret_rsem,
):
    cores, ys, zs = grid
    x = lax.axis_index("dp")
    e = lax.axis_index("expert")
    pair = (weight_pair(x, e % cores), e)
    twin = (weight_pair(x, 1 - e % cores), e)
    slabs, capacity, width = out_buf.shape
    per = slabs // 4
    rows = per * capacity
    columns = raw_in.shape[1]
    units = columns // 2
    padded = split_in.shape[1] // 2
    count = cores * ys * zs

    barrier = pltpu.get_barrier_semaphore()

    def greet(step, carry):
        pl.semaphore_signal(
            barrier, inc=1, device_id=(x, (e + step) % count), device_id_type=pl.DeviceIdType.MESH
        )
        return carry

    lax.fori_loop(1, count, greet, 0)
    pl.semaphore_signal(barrier, inc=1, device_id=pair, device_id_type=pl.DeviceIdType.MESH)
    pl.semaphore_signal(barrier, inc=1, device_id=twin, device_id_type=pl.DeviceIdType.MESH)

    def remote(src, dst, ssem, rsem, device):
        return pltpu.make_async_remote_copy(
            src_ref=src, dst_ref=dst, send_sem=ssem, recv_sem=rsem, device_id=device, device_id_type=pl.DeviceIdType.MESH
        )

    load_own = pltpu.make_async_copy(own_in, raw_in.at[0], local_sem.at[0])
    load_near = pltpu.make_async_copy(near_in, raw_in.at[1], local_sem.at[1])
    load_out = pltpu.make_async_copy(own_out, raw_out.at[0], local_sem.at[2])
    load_own.start()
    load_near.start()
    load_out.start()
    weight_out = remote(own_out, raw_out.at[1], weight_send, weight_recv, pair)

    def chunk_of(ref, c):
        return ref.at[pl.ds(c * per, per)]

    def pack_dispatch(c):
        picked = jnp.dot(dispatch[pl.ds(c * rows, rows), :], normed[...], preferred_element_type=f32)
        out_buf[pl.ds(c * per, per)] = picked.astype(bf16).reshape(per, capacity, width)

    def send_dispatch(c):
        def one(m, carry):
            index = c * per + m
            remote(
                out_buf.at[index], in_own.at[index], go_send.at[c], go_recv.at[c], (x, peer(e, index, 1, cores, ys, zs))
            ).start()
            return carry

        lax.fori_loop(jnp.where(c == 0, 1, 0), per, one, 0)

    def begin(c, carry):
        pack_dispatch(c)
        send_dispatch(c)
        return carry

    pack_dispatch(0)
    pl.semaphore_wait(barrier, count + 1)
    send_dispatch(0)
    weight_out.start()
    lax.fori_loop(1, 4, begin, 0)
    in_own[0] = out_buf[0]

    row = lax.broadcasted_iota(jnp.int32, (2 * padded, columns), 0)
    column = lax.broadcasted_iota(jnp.int32, (2 * padded, columns), 1)
    unit = jnp.where(row < padded, row, row - padded)
    wanted = jnp.where(unit < units, 2 * unit + jnp.where(row < padded, 0, 1), -1)
    part = (column == wanted).astype(f32).astype(bf16)

    def separate(k):
        for start in range(0, width, 768):
            cols = pl.ds(start, min(768, width - start))
            split_in[k, :, cols] = jnp.dot(part, raw_in[k, :, cols], preferred_element_type=f32).astype(bf16)

    load_own.wait()
    separate(0)
    load_near.wait()
    separate(1)
    load_out.wait()

    def wait_own(c):
        @pl.when(c == 0)
        def _():
            view = in_own.at[pl.ds(1, per - 1)]
            remote(view, view, go_send.at[0], go_recv.at[0], twin).wait_recv()

        @pl.when(c > 0)
        def _():
            view = chunk_of(in_own, c)
            remote(view, view, go_send.at[c], go_recv.at[c], twin).wait_recv()

    def forward(c):
        return remote(chunk_of(in_own, c), chunk_of(in_twin, c), twin_send.at[c], twin_recv.at[c], twin)

    def partial(c):
        return remote(chunk_of(part_send, c), chunk_of(part_recv, c), part_ssem.at[c], part_rsem.at[c], twin)

    def wait_sent(ref, sems, c):
        @pl.when(c == 0)
        def _():
            view = ref.at[pl.ds(1, per - 1)]
            remote(view, view, sems.at[0], go_recv.at[0], twin).wait_send()

        @pl.when(c > 0)
        def _():
            view = chunk_of(ref, c)
            remote(view, view, sems.at[c], go_recv.at[c], twin).wait_send()

    def compute(c):
        x_buf[pl.ds(0, rows), :] = in_own[pl.ds(c * per, per)].reshape(rows, width)
        x_buf[pl.ds(rows, rows), :] = in_twin[pl.ds(c * per, per)].reshape(rows, width)

        def units_of(k, carry):
            projected = lax.dot_general(
                x_buf[...], split_in[k], (((1,), (1,)), ((), ())), preferred_element_type=f32
            )
            gate = projected[:, :padded]
            up = projected[:, padded:]
            hidden = (up + 1.0) * gate * (1.0 / (1.0 + jnp.exp(-1.702 * gate)))
            h_buf[k] = hidden.astype(bf16)
            return carry

        lax.fori_loop(0, 2, units_of, 0)
        for start in range(0, width, 768):
            size = min(768, width - start)
            cols = pl.ds(start, size)
            total = jnp.dot(h_buf[0, :, :units], raw_out[0, :, cols], preferred_element_type=f32)
            total += jnp.dot(h_buf[1, :, :units], raw_out[1, :, cols], preferred_element_type=f32)
            own_part[c, :, cols] = total[:rows]
            part_send[pl.ds(c * per, per), :, cols] = total[rows:].astype(bf16).reshape(per, capacity, size)

    def give_back(c):
        wait_sent(out_buf, go_send, c)
        total = own_part[c] + part_recv[pl.ds(c * per, per)].astype(f32).reshape(rows, width)
        out_buf[pl.ds(c * per, per)] = total.astype(bf16).reshape(per, capacity, width)

        def one(m, carry):
            index = c * per + m
            remote(
                out_buf.at[index], ret_recv.at[index], ret_send.at[c], ret_rsem.at[c], (x, peer(e, index, -1, cores, ys, zs))
            ).start()
            return carry

        lax.fori_loop(jnp.where(c == 0, 1, 0), per, one, 0)

    def step(t, carry):
        @pl.when(t < 4)
        def _():
            wait_own(t)
            forward(t).start()

        @pl.when(t == 1)
        def _():
            weight_out.wait()

        @pl.when((t >= 1) & (t < 5))
        def _():
            forward(t - 1).wait_recv()
            compute(t - 1)
            partial(t - 1).start()

        @pl.when(t >= 2)
        def _():
            partial(t - 2).wait_recv()
            give_back(t - 2)

        return carry

    lax.fori_loop(0, 6, step, 0)
    ret_recv[0] = out_buf[0]

    def finish(c, carry):
        forward(c).wait_send()
        partial(c).wait_send()
        wait_sent(out_buf, ret_send, c)

        @pl.when(c == 0)
        def _():
            view = ret_recv.at[pl.ds(1, per - 1)]
            remote(view, view, go_send.at[0], ret_rsem.at[0], twin).wait_recv()

        @pl.when(c > 0)
        def _():
            view = chunk_of(ret_recv, c)
            remote(view, view, go_send.at[0], ret_rsem.at[c], twin).wait_recv()

        return carry

    lax.fori_loop(0, 4, finish, 0)
    for start in range(0, width, 768):
        size = min(768, width - start)
        cols = pl.ds(start, size)
        back = ret_recv[:, :, cols].reshape(slabs * capacity, size)
        mixed = jnp.dot(combine[0], back, preferred_element_type=f32)
        mixed += jnp.dot(combine[1], back, preferred_element_type=f32)
        result[:, cols] = (residual[:, cols] + mixed).astype(bf16)


def experts(grid, dispatch, normed, residual, combine, own_in, near_in, own_out):
    slots, row_count = dispatch.shape
    width = normed.shape[1]
    columns = own_in.shape[0]
    units = columns // 2
    padded = -(-units // 128) * 128
    slabs = grid[0] * grid[1] * grid[2]
    capacity = slots // slabs
    rows = slots // 4
    vmem = pl.BlockSpec(memory_space=pltpu.VMEM)
    hbm = pl.BlockSpec(memory_space=pl.ANY)
    dma = pltpu.SemaphoreType.DMA
    buffer = pltpu.VMEM((slabs, capacity, width), bf16)
    return pl.pallas_call(
        functools.partial(expert_kernel, grid),
        out_shape=jax.ShapeDtypeStruct((row_count, width), bf16),
        in_specs=[vmem, vmem, vmem, vmem, hbm, hbm, hbm],
        out_specs=vmem,
        scratch_shapes=[
            pltpu.VMEM((2, columns, width), bf16),
            pltpu.VMEM((2, 2 * padded, width), bf16),
            pltpu.VMEM((2, units, width), bf16),
            buffer,
            buffer,
            buffer,
            pltpu.VMEM((2 * rows, width), bf16),
            pltpu.VMEM((2, 2 * rows, padded), bf16),
            pltpu.VMEM((4, rows, width), f32),
            buffer,
            buffer,
            buffer,
            dma((3,)),
            dma,
            dma,
        ]
        + [dma((4,))] * 8,
        compiler_params=pltpu.CompilerParams(collective_id=1, has_side_effects=True, vmem_limit_bytes=60 << 20),
        cost_estimate=pl.CostEstimate(flops=14 << 30, bytes_accessed=30 << 20, transcendentals=0),
        name="experts",
    )(dispatch, normed, residual, combine, own_in, near_in, own_out)


def on_device(
    stream_rows,
    query_rows,
    key_value_rows,
    destination,
    lengths,
    out_weight,
    expert_index,
    router_weights,
    gate_up,
    down_weight,
):
    row_count, model_width = stream_rows.shape
    dp_count = lax.axis_size("dp")
    expert_count = lax.axis_size("expert")
    seq_len = row_count * dp_count
    my_block = lax.axis_index("dp")
    both = ("dp", "expert")
    cores, ys = 2, 4
    grid = (cores, ys, expert_count // (cores * ys))
    own_in = gate_up[0].T
    own_out = down_weight[0]
    swap = [
        (d * expert_count + e, weight_pair(d, e % cores) * expert_count + e)
        for d in range(dp_count)
        for e in range(expert_count)
    ]
    near_in = lax.ppermute(own_in, ("dp", "expert"), swap)

    share = row_count // expert_count
    row_id = jnp.arange(row_count, dtype=jnp.int32)
    pack = destination // seq_len
    rank = jnp.sum(
        ((pack[:, None] == pack[None, :]) & (row_id[None, :] < row_id[:, None])).astype(jnp.int32), axis=1
    )
    send_slot = pack * share + rank
    sender = (row_id[:, None] == send_slot[None, :]).astype(bf16)
    place = jnp.broadcast_to((destination % row_count).astype(bf16)[:, None], (row_count, 128))
    attention_rows = jnp.concatenate([query_rows, key_value_rows, place], axis=1)
    query_width = query_rows.shape[1]
    memory_width = key_value_rows.shape[1]

    def exchange(rows):
        width = rows.shape[1]
        moved = lax.all_to_all(
            pick(sender, rows).reshape(expert_count, share, width),
            "expert",
            split_axis=0,
            concat_axis=0,
            tiled=True,
        )
        return moved.reshape(row_count, width)

    got = exchange(attention_rows)
    got_stream = exchange(stream_rows)
    place_got = got[:, query_width + memory_width].astype(jnp.int32)
    settle = (row_id[:, None] == place_got[None, :]).astype(bf16)
    memory = pick(settle, got[:, query_width : query_width + memory_width])
    queries = pick(settle, got[:, :query_width])
    stream = jnp.dot(settle, got_stream, preferred_element_type=f32)

    group_size = HEADS // KV_HEADS
    key_width = KV_HEADS * HEAD_DIM
    seg_ends = jnp.cumsum(lengths[0])[:-1]
    query_position = my_block * row_count + row_id
    query_segment = segment_number(seg_ends, query_position)
    query_heads = queries.reshape(row_count, KV_HEADS, group_size, HEAD_DIM)

    def shift(value, step):
        if step == 0:
            return value
        return lax.ppermute(value, "dp", [(x, (x + step) % dp_count) for x in range(dp_count)])

    section = jnp.concatenate([shift(memory, s) for s in range(dp_count)], axis=0)
    key_position = jnp.concatenate(
        [lax.rem(my_block - s + dp_count, dp_count) * row_count + row_id for s in range(dp_count)]
    )
    key_count = section.shape[0]
    key_segment = segment_number(seg_ends, key_position)
    visible = (query_segment[:, None] == key_segment[None, :]) & (
        key_position[None, :] <= query_position[:, None]
    )
    key_block = section[:, :key_width].reshape(key_count, KV_HEADS, HEAD_DIM)
    value_block = section[:, key_width:].reshape(key_count, KV_HEADS, HEAD_DIM)
    scores = jnp.einsum(
        "tkgd,nkd->kgtn", query_heads, key_block, preferred_element_type=f32
    ) * HEAD_DIM ** (-0.5)
    scores = jnp.where(visible, scores, masked_score)
    row_max = jnp.max(scores, axis=-1)
    weights = jnp.where(visible, jnp.exp(scores - row_max[..., None]), 0.0)
    denominator = jnp.sum(weights, axis=-1)
    numerator = jnp.einsum(
        "kgtn,nkd->kgtd", weights.astype(bf16), value_block, preferred_element_type=f32
    )
    context = (
        (numerator / denominator[..., None])
        .transpose(2, 0, 1, 3)
        .reshape(row_count, HEADS * HEAD_DIM)
        .astype(bf16)
    )
    parts = []
    for s in range(dp_count):
        part = jnp.dot(shift(context, s), out_weight, preferred_element_type=f32).astype(bf16)
        parts.append(shift(part, (dp_count - s) % dp_count))
    order = lax.rem(jnp.arange(dp_count, dtype=jnp.int32) - my_block + dp_count, dp_count)
    update = jnp.stack(parts)[order].transpose(1, 0, 2).reshape(row_count, model_width)
    residual = stream + update.astype(f32)
    normed = (
        residual * lax.rsqrt(jnp.mean(residual * residual, axis=-1, keepdims=True) + norm_eps)
    ).astype(bf16)

    entry_count = row_count * TOPK
    capacity = entry_count // expert_count
    flat_index = expert_index.reshape(entry_count)
    onehot = (flat_index[:, None] == jnp.arange(expert_count, dtype=jnp.int32)[None, :]).astype(
        jnp.int32
    )
    slot_index = jnp.sum(onehot * (jnp.cumsum(onehot, axis=0) - 1), axis=1)
    kept_mask = slot_index < capacity
    slots = expert_count * capacity
    slab = jnp.arange(expert_count, dtype=jnp.int32)
    holder = peer(lax.axis_index("expert"), slab, 1, *grid)
    slab_expert = jnp.repeat(holder, capacity)
    slab_slot = jnp.tile(jnp.arange(capacity, dtype=jnp.int32), expert_count)
    slot_id = slab_expert * capacity + slab_slot
    target = jnp.where(kept_mask, flat_index * capacity + slot_index, slots).reshape(row_count, TOPK)
    dispatch = jnp.zeros((slots, row_count), f32)
    combine = jnp.zeros((row_count, slots), f32)
    entry_weight = router_weights.reshape(row_count, TOPK)
    for k in range(TOPK):
        dispatch = dispatch + (slot_id[:, None] == target[None, :, k]).astype(f32)
        combine = combine + jnp.where(target[:, k, None] == slot_id[None, :], entry_weight[:, k, None], 0.0)
    high = lax.reduce_precision(combine, 8, 7)
    low = (combine - high).astype(bf16)
    combine = jnp.stack([high.astype(bf16), low])
    scored = experts(grid, dispatch.astype(bf16), normed, residual, combine, own_in, near_in, own_out)
    return scored.reshape(1, row_count, model_width)


def solution(mesh):
    placed = (
        P(("dp", "expert"), None),
        P(("dp", "expert"), None),
        P(("dp", "expert"), None),
        P(("dp", "expert")),
        P("expert", None),
        P(None, "dp"),
        P("expert", "dp", None),
        P("expert", "dp", None),
        P("expert", None, "dp"),
        P("expert", "dp", None),
    )
    return jax.shard_map(
        on_device, mesh=mesh, in_specs=placed, out_specs=P("expert", "dp", None), check_vma=False
    )
```

```python
import functools

import jax
import jax.numpy as jnp
from jax import lax
from jax.experimental import pallas as pl
from jax.experimental.pallas import tpu as pltpu
from jax.sharding import PartitionSpec as P

HEADS = 32
KV_HEADS = 4
HEAD_DIM = 64
TOPK = 4


masked_score = -1e30
norm_eps = 1e-05
f32 = jnp.float32
bf16 = jnp.bfloat16


def segment_number(seg_ends, positions):
    return jnp.sum((positions[:, None] >= seg_ends[None, :]).astype(jnp.int32), axis=1)


def relation(index, cores, ys, zs):
    per = zs * cores
    half = max(zs // 2, 1)
    chunk, rest = index // per, index % per
    turn = rest // cores
    dz = (turn % 2) * (half + turn // 2) + (1 - turn % 2) * ((half - turn // 2) % half)
    return dz, (chunk + zs * ys - dz) % ys, rest % cores


def peer(expert, index, sign, cores, ys, zs):
    dz, dy, dc = relation(index, cores, ys, zs)
    z, y, c = expert // (ys * cores), (expert // cores) % ys, expert % cores
    z = (z + sign * dz + zs) % zs
    y = (y + sign * dy + ys) % ys
    c = (c + dc) % cores
    return (z * ys + y) * cores + c


def weight_pair(x, core):
    return (x + 5 - 2 * ((x + core) % 2)) % 4


def expert_kernel(
    grid,
    dispatch,
    normed,
    residual,
    combine,
    own_in,
    near_in,
    own_out,
    result,
    raw_in,
    split_in,
    raw_out,
    out_buf,
    in_own,
    in_twin,
    x_buf,
    h_buf,
    own_part,
    part_send,
    part_recv,
    ret_recv,
    local_sem,
    weight_send,
    weight_recv,
    go_send,
    go_recv,
    twin_send,
    twin_recv,
    part_ssem,
    part_rsem,
    ret_send,
    ret_rsem,
):
    cores, ys, zs = grid
    x = lax.axis_index("dp")
    e = lax.axis_index("expert")
    pair = (weight_pair(x, e % cores), e)
    twin = (weight_pair(x, 1 - e % cores), e)
    slabs, capacity, width = out_buf.shape
    per = slabs // 4
    rows = per * capacity
    columns = raw_in.shape[1]
    units = columns // 2
    padded = split_in.shape[1] // 2
    count = cores * ys * zs

    barrier = pltpu.get_barrier_semaphore()

    def greet(step, carry):
        pl.semaphore_signal(
            barrier, inc=1, device_id=(x, (e + step) % count), device_id_type=pl.DeviceIdType.MESH
        )
        return carry

    lax.fori_loop(1, count, greet, 0)
    pl.semaphore_signal(barrier, inc=1, device_id=pair, device_id_type=pl.DeviceIdType.MESH)
    pl.semaphore_signal(barrier, inc=1, device_id=twin, device_id_type=pl.DeviceIdType.MESH)

    def remote(src, dst, ssem, rsem, device):
        return pltpu.make_async_remote_copy(
            src_ref=src, dst_ref=dst, send_sem=ssem, recv_sem=rsem, device_id=device, device_id_type=pl.DeviceIdType.MESH
        )

    load_own = pltpu.make_async_copy(own_in, raw_in.at[0], local_sem.at[0])
    load_near = pltpu.make_async_copy(near_in, raw_in.at[1], local_sem.at[1])
    load_out = pltpu.make_async_copy(own_out, raw_out.at[0], local_sem.at[2])
    load_own.start()
    load_near.start()
    load_out.start()
    weight_out = remote(own_out, raw_out.at[1], weight_send, weight_recv, pair)

    def chunk_of(ref, c):
        return ref.at[pl.ds(c * per, per)]

    def pack_dispatch(c):
        picked = jnp.dot(dispatch[pl.ds(c * rows, rows), :], normed[...], preferred_element_type=f32)
        out_buf[pl.ds(c * per, per)] = picked.astype(bf16).reshape(per, capacity, width)

    def send_dispatch(c):
        def one(m, carry):
            index = c * per + m
            remote(
                out_buf.at[index], in_own.at[index], go_send.at[c], go_recv.at[c], (x, peer(e, index, 1, cores, ys, zs))
            ).start()
            return carry

        lax.fori_loop(jnp.where(c == 0, 1, 0), per, one, 0)

    def begin(c, carry):
        pack_dispatch(c)
        send_dispatch(c)
        return carry

    pack_dispatch(0)
    pl.semaphore_wait(barrier, count + 1)
    send_dispatch(0)
    weight_out.start()
    lax.fori_loop(1, 4, begin, 0)
    in_own[0] = out_buf[0]

    row = lax.broadcasted_iota(jnp.int32, (2 * padded, columns), 0)
    column = lax.broadcasted_iota(jnp.int32, (2 * padded, columns), 1)
    unit = jnp.where(row < padded, row, row - padded)
    wanted = jnp.where(unit < units, 2 * unit + jnp.where(row < padded, 0, 1), -1)
    part = (column == wanted).astype(f32).astype(bf16)

    def separate(k):
        for start in range(0, width, 768):
            cols = pl.ds(start, min(768, width - start))
            split_in[k, :, cols] = jnp.dot(part, raw_in[k, :, cols], preferred_element_type=f32).astype(bf16)

    load_own.wait()
    separate(0)
    load_near.wait()
    separate(1)
    load_out.wait()

    def wait_own(c):
        @pl.when(c == 0)
        def _():
            view = in_own.at[pl.ds(1, per - 1)]
            remote(view, view, go_send.at[0], go_recv.at[0], twin).wait_recv()

        @pl.when(c > 0)
        def _():
            view = chunk_of(in_own, c)
            remote(view, view, go_send.at[c], go_recv.at[c], twin).wait_recv()

    def forward(c):
        return remote(chunk_of(in_own, c), chunk_of(in_twin, c), twin_send.at[c], twin_recv.at[c], twin)

    def partial(c):
        return remote(chunk_of(part_send, c), chunk_of(part_recv, c), part_ssem.at[c], part_rsem.at[c], twin)

    def wait_sent(ref, sems, c):
        @pl.when(c == 0)
        def _():
            view = ref.at[pl.ds(1, per - 1)]
            remote(view, view, sems.at[0], go_recv.at[0], twin).wait_send()

        @pl.when(c > 0)
        def _():
            view = chunk_of(ref, c)
            remote(view, view, sems.at[c], go_recv.at[c], twin).wait_send()

    def compute(c):
        x_buf[pl.ds(0, rows), :] = in_own[pl.ds(c * per, per)].reshape(rows, width)
        x_buf[pl.ds(rows, rows), :] = in_twin[pl.ds(c * per, per)].reshape(rows, width)

        def units_of(k, carry):
            projected = lax.dot_general(
                x_buf[...], split_in[k], (((1,), (1,)), ((), ())), preferred_element_type=f32
            )
            gate = projected[:, :padded]
            up = projected[:, padded:]
            hidden = (up + 1.0) * gate * (1.0 / (1.0 + jnp.exp(-1.702 * gate)))
            h_buf[k] = hidden.astype(bf16)
            return carry

        lax.fori_loop(0, 2, units_of, 0)
        for start in range(0, width, 768):
            size = min(768, width - start)
            cols = pl.ds(start, size)
            total = jnp.dot(h_buf[0, :, :units], raw_out[0, :, cols], preferred_element_type=f32)
            total += jnp.dot(h_buf[1, :, :units], raw_out[1, :, cols], preferred_element_type=f32)
            own_part[c, :, cols] = total[:rows]
            part_send[pl.ds(c * per, per), :, cols] = total[rows:].astype(bf16).reshape(per, capacity, size)

    def give_back(c):
        wait_sent(out_buf, go_send, c)
        total = own_part[c] + part_recv[pl.ds(c * per, per)].astype(f32).reshape(rows, width)
        out_buf[pl.ds(c * per, per)] = total.astype(bf16).reshape(per, capacity, width)

        def one(m, carry):
            index = c * per + m
            remote(
                out_buf.at[index], ret_recv.at[index], ret_send.at[c], ret_rsem.at[c], (x, peer(e, index, -1, cores, ys, zs))
            ).start()
            return carry

        lax.fori_loop(jnp.where(c == 0, 1, 0), per, one, 0)

    def step(t, carry):
        @pl.when(t < 4)
        def _():
            wait_own(t)
            forward(t).start()

        @pl.when(t == 1)
        def _():
            weight_out.wait()

        @pl.when((t >= 1) & (t < 5))
        def _():
            forward(t - 1).wait_recv()
            compute(t - 1)
            partial(t - 1).start()

        @pl.when(t >= 2)
        def _():
            partial(t - 2).wait_recv()
            give_back(t - 2)

        return carry

    lax.fori_loop(0, 6, step, 0)
    ret_recv[0] = out_buf[0]

    def finish(c, carry):
        forward(c).wait_send()
        partial(c).wait_send()
        wait_sent(out_buf, ret_send, c)

        @pl.when(c == 0)
        def _():
            view = ret_recv.at[pl.ds(1, per - 1)]
            remote(view, view, go_send.at[0], ret_rsem.at[0], twin).wait_recv()

        @pl.when(c > 0)
        def _():
            view = chunk_of(ret_recv, c)
            remote(view, view, go_send.at[0], ret_rsem.at[c], twin).wait_recv()

        return carry

    lax.fori_loop(0, 4, finish, 0)
    for start in range(0, width, 768):
        size = min(768, width - start)
        cols = pl.ds(start, size)
        back = ret_recv[:, :, cols].reshape(slabs * capacity, size)
        mixed = jnp.dot(combine[0], back, preferred_element_type=f32)
        mixed += jnp.dot(combine[1], back, preferred_element_type=f32)
        result[:, cols] = (residual[:, cols] + mixed).astype(bf16)


def experts(grid, dispatch, normed, residual, combine, own_in, near_in, own_out):
    slots, row_count = dispatch.shape
    width = normed.shape[1]
    columns = own_in.shape[0]
    units = columns // 2
    padded = -(-units // 128) * 128
    slabs = grid[0] * grid[1] * grid[2]
    capacity = slots // slabs
    rows = slots // 4
    vmem = pl.BlockSpec(memory_space=pltpu.VMEM)
    hbm = pl.BlockSpec(memory_space=pl.ANY)
    dma = pltpu.SemaphoreType.DMA
    buffer = pltpu.VMEM((slabs, capacity, width), bf16)
    return pl.pallas_call(
        functools.partial(expert_kernel, grid),
        out_shape=jax.ShapeDtypeStruct((row_count, width), bf16),
        in_specs=[vmem, vmem, vmem, vmem, hbm, hbm, hbm],
        out_specs=vmem,
        scratch_shapes=[
            pltpu.VMEM((2, columns, width), bf16),
            pltpu.VMEM((2, 2 * padded, width), bf16),
            pltpu.VMEM((2, units, width), bf16),
            buffer,
            buffer,
            buffer,
            pltpu.VMEM((2 * rows, width), bf16),
            pltpu.VMEM((2, 2 * rows, padded), bf16),
            pltpu.VMEM((4, rows, width), f32),
            buffer,
            buffer,
            buffer,
            dma((3,)),
            dma,
            dma,
        ]
        + [dma((4,))] * 8,
        compiler_params=pltpu.CompilerParams(collective_id=1, has_side_effects=True, vmem_limit_bytes=60 << 20),
        cost_estimate=pl.CostEstimate(flops=14 << 30, bytes_accessed=30 << 20, transcendentals=0),
        name="experts",
    )(dispatch, normed, residual, combine, own_in, near_in, own_out)


PIECE = 384
PIECES = 8


def attention_kernel(
    grid,
    sender,
    place,
    stream_t,
    query,
    key_value,
    visible,
    weight_hbm,
    residual,
    normed,
    weight_t,
    shuffle,
    stack,
    early_out,
    early_in,
    late_out,
    late_in,
    sorted_rows,
    section,
    context,
    parts,
    columns,
    local_sem,
    early_send,
    early_recv,
    late_send,
    late_recv,
    key_send,
    key_recv,
    context_send,
    context_recv,
    column_send,
    column_recv,
):
    cores, ys, zs = grid
    x = lax.axis_index("dp")
    e = lax.axis_index("expert")
    count = cores * ys * zs
    rows = sender.shape[0]
    share = rows // count
    width = residual.shape[1]
    slab = PIECES * share
    mesh_id = pl.DeviceIdType.MESH

    def remote(src, dst, ssem, rsem, device):
        return pltpu.make_async_remote_copy(
            src_ref=src, dst_ref=dst, send_sem=ssem, recv_sem=rsem, device_id=device, device_id_type=mesh_id
        )

    barrier = pltpu.get_barrier_semaphore()

    def greet(step, carry):
        pl.semaphore_signal(barrier, inc=1, device_id=(x, (e + step) % count), device_id_type=mesh_id)
        return carry

    lax.fori_loop(1, count, greet, 0)
    for s in range(1, 4):
        pl.semaphore_signal(barrier, inc=1, device_id=((x + s) % 4, e), device_id_type=mesh_id)
    load = pltpu.make_async_copy(weight_hbm, weight_t, local_sem)
    load.start()

    size = count * slab
    row = lax.broadcasted_iota(jnp.int32, (size, 1), 0)
    column = lax.broadcasted_iota(jnp.int32, (size, size), 1)
    source = (row % slab) // share * rows + row // slab * share + row % share
    shuffle[0] = (column == source).astype(f32).astype(bf16)
    source = (row % rows) // share * slab + row // rows * share + row % share
    shuffle[1] = (column == source).astype(f32).astype(bf16)

    def pack(values, out):
        stack[...] = jnp.zeros_like(stack)
        for start, value in values:
            done = 0
            while done < value.shape[1]:
                piece, offset = (start + done) // PIECE, (start + done) % PIECE
                part = min(PIECE - offset, value.shape[1] - done)
                stack[pl.ds(piece * rows, rows), pl.ds(offset, part)] = value[:, done : done + part]
                done += part
        out[...] = (
            jnp.dot(shuffle[0], stack[...], preferred_element_type=f32).astype(bf16).reshape(count, slab, PIECE)
        )

    def unpack(got):
        stack[...] = jnp.dot(
            shuffle[1], got[...].reshape(size, PIECE), preferred_element_type=f32
        ).astype(bf16)

    def send_all(src, dst, ssem, rsem):
        def one(index, carry):
            remote(src.at[index], dst.at[index], ssem, rsem, (x, peer(e, index, 1, cores, ys, zs))).start()
            return carry

        lax.fori_loop(1, count, one, 0)
        dst[0] = src[0]

    def all_of(src, dst, ssem, rsem):
        return remote(src.at[pl.ds(1, count - 1)], dst.at[pl.ds(1, count - 1)], ssem, rsem, (x, (e + 1) % count))

    query_width, memory_width = query.shape[1], key_value.shape[1]
    early_width = query_width + memory_width
    pack(
        [
            (0, jnp.dot(sender[...], query[...], preferred_element_type=f32).astype(bf16)),
            (query_width, jnp.dot(sender[...], key_value[...], preferred_element_type=f32).astype(bf16)),
            (early_width, jnp.dot(sender[...], place[...], preferred_element_type=f32).astype(bf16)),
        ],
        early_out,
    )
    pl.semaphore_wait(barrier, count + 2)
    send_all(early_out, early_in, early_send, early_recv)
    pack(
        [
            (
                0,
                lax.dot_general(
                    sender[...], stream_t[...], (((1,), (1,)), ((), ())), preferred_element_type=f32
                ).astype(bf16),
            )
        ],
        late_out,
    )
    send_all(late_out, late_in, late_send, late_recv)

    all_of(early_out, early_in, early_send, early_recv).wait_recv()
    unpack(early_in)
    last, offset = early_width // PIECE, early_width % PIECE
    spots = stack[pl.ds(last * rows, rows), pl.ds(offset, 128)].astype(f32)
    settle = jnp.transpose(spots)[:rows].astype(bf16)
    for piece in range(last + 1):
        part = min(PIECE, early_width - piece * PIECE)
        moved = jnp.dot(settle, stack[pl.ds(piece * rows, rows), :], preferred_element_type=f32).astype(bf16)
        sorted_rows[:, pl.ds(piece * PIECE, part)] = moved[:, :part]
    section[0] = sorted_rows[:, pl.ds(query_width, memory_width)]
    for s in range(1, 4):
        remote(section.at[0], section.at[s], key_send, key_recv, ((x + s) % 4, e)).start()

    keys = remote(section.at[pl.ds(1, 3)], section.at[pl.ds(1, 3)], key_send, key_recv, ((x + 1) % 4, e))
    keys.wait_recv()
    key_count = 4 * rows
    group = HEADS // KV_HEADS
    key_width = KV_HEADS * HEAD_DIM
    for h in range(KV_HEADS):
        key = section[:, :, h * HEAD_DIM : (h + 1) * HEAD_DIM].reshape(key_count, HEAD_DIM)
        value = section[:, :, key_width + h * HEAD_DIM : key_width + (h + 1) * HEAD_DIM].reshape(
            key_count, HEAD_DIM
        )
        head_rows = jnp.concatenate(
            [
                sorted_rows[:, (h * group + g) * HEAD_DIM : (h * group + g + 1) * HEAD_DIM]
                for g in range(group)
            ],
            axis=0,
        )
        scores = lax.dot_general(
            head_rows, key, (((1,), (1,)), ((), ())), preferred_element_type=f32
        ) * HEAD_DIM ** (-0.5)
        seen = (visible[...] > 0.0)[None]
        scores = jnp.where(seen, scores.reshape(group, rows, key_count), masked_score)
        top = jnp.max(scores, axis=-1, keepdims=True)
        weights = jnp.where(seen, jnp.exp(scores - top), 0.0)
        denominator = jnp.sum(weights, axis=-1, keepdims=True)
        numerator = jnp.dot(
            weights.astype(bf16).reshape(group * rows, key_count), value, preferred_element_type=f32
        ).reshape(group, rows, HEAD_DIM)
        heads = (numerator / denominator).astype(bf16)
        context[0, h] = jnp.concatenate([heads[g] for g in range(group)], axis=1)
        for s in (2, 1, 3):
            remote(
                context.at[0, h], context.at[s, h], context_send.at[s - 1], context_recv.at[s - 1], ((x + s) % 4, e)
            ).start()

    load.wait()
    depth = group * HEAD_DIM

    def project(s):
        total = None
        for h in range(KV_HEADS):
            term = lax.dot_general(
                context[s, h],
                weight_t[:, pl.ds(h * depth, depth)],
                (((1,), (1,)), ((), ())),
                preferred_element_type=f32,
            )
            total = term if total is None else total + term
        return total.astype(bf16)

    def whole_context(s):
        return remote(
            context.at[0], context.at[s], context_send.at[s - 1], context_recv.at[s - 1], ((x + s) % 4, e)
        )

    columns[x] = project(0)
    all_of(late_out, late_in, late_send, late_recv).wait_recv()
    unpack(late_in)
    for start in range(0, width, PIECE):
        part = min(PIECE, width - start)
        moved = jnp.dot(
            settle, stack[pl.ds(start // PIECE * rows, rows), :], preferred_element_type=f32
        )
        residual[:, pl.ds(start, part)] = moved[:, :part]
    for s in (1, 3, 2):
        whole_context(s).wait_recv()
        parts[s - 1] = project(s)
        remote(parts.at[s - 1], columns.at[x], column_send, column_recv, ((x + 4 - s) % 4, e)).start()
    done = remote(parts, columns.at[pl.ds(0, 3)], column_send, column_recv, ((x + 1) % 4, e))
    done.wait_recv()
    update = jnp.concatenate([columns[d] for d in range(4)], axis=1).astype(f32)
    total = residual[...] + update
    residual[...] = total
    scale = lax.rsqrt(jnp.mean(total * total, axis=-1, keepdims=True) + norm_eps)
    normed[...] = (total * scale).astype(bf16)
    done.wait_send()
    keys.wait_send()
    for s in range(1, 4):
        whole_context(s).wait_send()
    all_of(early_out, early_in, early_send, early_recv).wait_send()
    all_of(late_out, late_in, late_send, late_recv).wait_send()


def attend(grid, sender, place, stream_t, query, key_value, visible, weight_t):
    rows = sender.shape[0]
    width = stream_t.shape[0]
    count = grid[0] * grid[1] * grid[2]
    slab = PIECES * (rows // count)
    size = count * slab
    vmem = pl.BlockSpec(memory_space=pltpu.VMEM)
    hbm = pl.BlockSpec(memory_space=pl.ANY)
    dma = pltpu.SemaphoreType.DMA
    slabs = pltpu.VMEM((count, slab, PIECE), bf16)
    early_width = query.shape[1] + key_value.shape[1]
    return pl.pallas_call(
        functools.partial(attention_kernel, grid),
        out_shape=[jax.ShapeDtypeStruct((rows, width), f32), jax.ShapeDtypeStruct((rows, width), bf16)],
        in_specs=[vmem] * 6 + [hbm],
        out_specs=[vmem, vmem],
        scratch_shapes=[
            pltpu.VMEM(weight_t.shape, bf16),
            pltpu.VMEM((2, size, size), bf16),
            pltpu.VMEM((size, PIECE), bf16),
            slabs,
            slabs,
            slabs,
            slabs,
            pltpu.VMEM((rows, early_width), bf16),
            pltpu.VMEM((4, rows, key_value.shape[1]), bf16),
            pltpu.VMEM((4, KV_HEADS, rows, HEADS // KV_HEADS * HEAD_DIM), bf16),
            pltpu.VMEM((3, rows, width // 4), bf16),
            pltpu.VMEM((4, rows, width // 4), bf16),
            dma,
            dma,
            dma,
            dma,
            dma,
            dma,
            dma,
            dma((3,)),
            dma((3,)),
            dma,
            dma,
        ],
        compiler_params=pltpu.CompilerParams(
            collective_id=2, has_side_effects=True, vmem_limit_bytes=60 << 20
        ),
        cost_estimate=pl.CostEstimate(flops=5 << 30, bytes_accessed=8 << 20, transcendentals=0),
        name="attend",
    )(sender, place, stream_t, query, key_value, visible, weight_t)


def on_device(
    stream_rows,
    query_rows,
    key_value_rows,
    destination,
    lengths,
    out_weight,
    expert_index,
    router_weights,
    gate_up,
    down_weight,
):
    row_count, model_width = stream_rows.shape
    dp_count = lax.axis_size("dp")
    expert_count = lax.axis_size("expert")
    seq_len = row_count * dp_count
    my_block = lax.axis_index("dp")
    both = ("dp", "expert")
    cores, ys = 2, 4
    grid = (cores, ys, expert_count // (cores * ys))
    own_in = gate_up[0].T
    own_out = down_weight[0]
    swap = [
        (d * expert_count + e, weight_pair(d, e % cores) * expert_count + e)
        for d in range(dp_count)
        for e in range(expert_count)
    ]
    near_in = lax.ppermute(own_in, ("dp", "expert"), swap)

    share = row_count // expert_count
    row_id = jnp.arange(row_count, dtype=jnp.int32)
    pack = destination // seq_len
    rank = jnp.sum(
        ((pack[:, None] == pack[None, :]) & (row_id[None, :] < row_id[:, None])).astype(jnp.int32), axis=1
    )
    send_slot = pack * share + rank
    slab = jnp.arange(expert_count, dtype=jnp.int32)
    holder = peer(lax.axis_index("expert"), slab, 1, *grid)
    slot_of = jnp.repeat(holder, share) * share + jnp.tile(jnp.arange(share, dtype=jnp.int32), expert_count)
    sender = (slot_of[:, None] == send_slot[None, :]).astype(bf16)
    lane = jnp.arange(128, dtype=jnp.int32)
    place = ((destination % row_count)[:, None] == lane[None, :]).astype(bf16)
    seg_ends = jnp.cumsum(lengths[0])[:-1]
    query_position = my_block * row_count + row_id
    query_segment = segment_number(seg_ends, query_position)
    key_position = jnp.concatenate(
        [lax.rem(my_block - s + dp_count, dp_count) * row_count + row_id for s in range(dp_count)]
    )
    key_segment = segment_number(seg_ends, key_position)
    visible = (query_segment[:, None] == key_segment[None, :]) & (
        key_position[None, :] <= query_position[:, None]
    )
    residual, normed = attend(
        grid, sender, place, stream_rows.T, query_rows, key_value_rows, visible.astype(f32), out_weight.T
    )

    entry_count = row_count * TOPK
    capacity = entry_count // expert_count
    flat_index = expert_index.reshape(entry_count)
    onehot = (flat_index[:, None] == jnp.arange(expert_count, dtype=jnp.int32)[None, :]).astype(
        jnp.int32
    )
    slot_index = jnp.sum(onehot * (jnp.cumsum(onehot, axis=0) - 1), axis=1)
    kept_mask = slot_index < capacity
    slots = expert_count * capacity
    slab_expert = jnp.repeat(holder, capacity)
    slab_slot = jnp.tile(jnp.arange(capacity, dtype=jnp.int32), expert_count)
    slot_id = slab_expert * capacity + slab_slot
    target = jnp.where(kept_mask, flat_index * capacity + slot_index, slots).reshape(row_count, TOPK)
    dispatch = jnp.zeros((slots, row_count), f32)
    combine = jnp.zeros((row_count, slots), f32)
    entry_weight = router_weights.reshape(row_count, TOPK)
    for k in range(TOPK):
        dispatch = dispatch + (slot_id[:, None] == target[None, :, k]).astype(f32)
        combine = combine + jnp.where(target[:, k, None] == slot_id[None, :], entry_weight[:, k, None], 0.0)
    high = lax.reduce_precision(combine, 8, 7)
    low = (combine - high).astype(bf16)
    combine = jnp.stack([high.astype(bf16), low])
    scored = experts(grid, dispatch.astype(bf16), normed, residual, combine, own_in, near_in, own_out)
    return scored.reshape(1, row_count, model_width)


def solution(mesh):
    placed = (
        P(("dp", "expert"), None),
        P(("dp", "expert"), None),
        P(("dp", "expert"), None),
        P(("dp", "expert")),
        P("expert", None),
        P(None, "dp"),
        P("expert", "dp", None),
        P("expert", "dp", None),
        P("expert", None, "dp"),
        P("expert", "dp", None),
    )
    return jax.shard_map(
        on_device, mesh=mesh, in_specs=placed, out_specs=P("expert", "dp", None), check_vma=False
    )
```

```python
import functools

import jax
import jax.numpy as jnp
from jax import lax
from jax.experimental import pallas as pl
from jax.experimental.pallas import tpu as pltpu
from jax.sharding import PartitionSpec as P

HEADS = 32
KV_HEADS = 4
HEAD_DIM = 64
TOPK = 4


masked_score = -1e30
norm_eps = 1e-05
f32 = jnp.float32
bf16 = jnp.bfloat16


def relation(index, cores, ys, zs):
    per = zs * cores
    half = max(zs // 2, 1)
    chunk, rest = index // per, index % per
    turn = rest // cores
    dz = (turn % 2) * (half + turn // 2) + (1 - turn % 2) * ((half - turn // 2) % half)
    return dz, (chunk + zs * ys - dz) % ys, rest % cores


def peer(expert, index, sign, cores, ys, zs):
    dz, dy, dc = relation(index, cores, ys, zs)
    z, y, c = expert // (ys * cores), (expert // cores) % ys, expert % cores
    z = (z + sign * dz + zs) % zs
    y = (y + sign * dy + ys) % ys
    c = (c + dc) % cores
    return (z * ys + y) * cores + c


def weight_pair(x, core):
    return (x + 5 - 2 * ((x + core) % 2)) % 4


def expert_kernel(
    grid,
    dispatch,
    normed,
    residual,
    combine,
    own_in,
    near_in,
    own_out,
    result,
    raw_in,
    split_in,
    raw_out,
    out_buf,
    in_own,
    in_twin,
    x_buf,
    h_buf,
    own_part,
    part_send,
    part_recv,
    ret_recv,
    local_sem,
    weight_send,
    weight_recv,
    go_send,
    go_recv,
    twin_send,
    twin_recv,
    part_ssem,
    part_rsem,
    ret_send,
    ret_rsem,
):
    cores, ys, zs = grid
    x = lax.axis_index("dp")
    e = lax.axis_index("expert")
    pair = (weight_pair(x, e % cores), e)
    twin = (weight_pair(x, 1 - e % cores), e)
    slabs, capacity, width = out_buf.shape
    per = slabs // 4
    rows = per * capacity
    columns = raw_in.shape[1]
    units = columns // 2
    padded = split_in.shape[1] // 2
    count = cores * ys * zs

    barrier = pltpu.get_barrier_semaphore()

    def greet(step, carry):
        pl.semaphore_signal(
            barrier, inc=1, device_id=(x, (e + step) % count), device_id_type=pl.DeviceIdType.MESH
        )
        return carry

    lax.fori_loop(1, count, greet, 0)
    pl.semaphore_signal(barrier, inc=1, device_id=pair, device_id_type=pl.DeviceIdType.MESH)
    pl.semaphore_signal(barrier, inc=1, device_id=twin, device_id_type=pl.DeviceIdType.MESH)

    def remote(src, dst, ssem, rsem, device):
        return pltpu.make_async_remote_copy(
            src_ref=src, dst_ref=dst, send_sem=ssem, recv_sem=rsem, device_id=device, device_id_type=pl.DeviceIdType.MESH
        )

    load_own = pltpu.make_async_copy(own_in, raw_in.at[0], local_sem.at[0])
    load_near = pltpu.make_async_copy(near_in, raw_in.at[1, pl.ds(0, near_in.shape[0])], local_sem.at[1])
    load_out = pltpu.make_async_copy(own_out, raw_out.at[0], local_sem.at[2])
    load_own.start()
    load_near.start()
    load_out.start()
    sent = near_in.shape[0]
    rest = pl.ds(sent, columns - sent)
    weight_in = remote(own_in.at[rest], raw_in.at[1, rest], weight_send.at[0], weight_recv.at[0], pair)
    weight_out = remote(own_out, raw_out.at[1], weight_send.at[1], weight_recv.at[1], pair)

    def chunk_of(ref, c):
        return ref.at[pl.ds(c * per, per)]

    def pack_dispatch(c):
        picked = jnp.dot(dispatch[pl.ds(c * rows, rows), :], normed[...], preferred_element_type=f32)
        out_buf[pl.ds(c * per, per)] = picked.astype(bf16).reshape(per, capacity, width)

    def send_dispatch(c):
        def one(m, carry):
            index = c * per + m
            remote(
                out_buf.at[index], in_own.at[index], go_send.at[c], go_recv.at[c], (x, peer(e, index, 1, cores, ys, zs))
            ).start()
            return carry

        lax.fori_loop(jnp.where(c == 0, 1, 0), per, one, 0)

    def begin(c, carry):
        pack_dispatch(c)
        send_dispatch(c)
        return carry

    pack_dispatch(0)
    pl.semaphore_wait(barrier, count + 1)
    send_dispatch(0)
    weight_in.start()
    weight_out.start()
    lax.fori_loop(1, 4, begin, 0)
    in_own[0] = out_buf[0]

    row = lax.broadcasted_iota(jnp.int32, (2 * padded, columns), 0)
    column = lax.broadcasted_iota(jnp.int32, (2 * padded, columns), 1)
    unit = jnp.where(row < padded, row, row - padded)
    wanted = jnp.where(unit < units, 2 * unit + jnp.where(row < padded, 0, 1), -1)
    part = (column == wanted).astype(f32).astype(bf16)

    def separate(k):
        for start in range(0, width, 768):
            cols = pl.ds(start, min(768, width - start))
            split_in[k, :, cols] = jnp.dot(part, raw_in[k, :, cols], preferred_element_type=f32).astype(bf16)

    load_own.wait()
    separate(0)
    load_near.wait()
    load_out.wait()

    def wait_own(c):
        @pl.when(c == 0)
        def _():
            view = in_own.at[pl.ds(1, per - 1)]
            remote(view, view, go_send.at[0], go_recv.at[0], twin).wait_recv()

        @pl.when(c > 0)
        def _():
            view = chunk_of(in_own, c)
            remote(view, view, go_send.at[c], go_recv.at[c], twin).wait_recv()

    def forward(c):
        return remote(chunk_of(in_own, c), chunk_of(in_twin, c), twin_send.at[c], twin_recv.at[c], twin)

    def partial(c):
        return remote(chunk_of(part_send, c), chunk_of(part_recv, c), part_ssem.at[c], part_rsem.at[c], twin)

    def wait_sent(ref, sems, c):
        @pl.when(c == 0)
        def _():
            view = ref.at[pl.ds(1, per - 1)]
            remote(view, view, sems.at[0], go_recv.at[0], twin).wait_send()

        @pl.when(c > 0)
        def _():
            view = chunk_of(ref, c)
            remote(view, view, sems.at[c], go_recv.at[c], twin).wait_send()

    def compute(c):
        x_buf[pl.ds(0, rows), :] = in_own[pl.ds(c * per, per)].reshape(rows, width)
        x_buf[pl.ds(rows, rows), :] = in_twin[pl.ds(c * per, per)].reshape(rows, width)

        def units_of(k, carry):
            projected = lax.dot_general(
                x_buf[...], split_in[k], (((1,), (1,)), ((), ())), preferred_element_type=f32
            )
            gate = projected[:, :padded]
            up = projected[:, padded:]
            hidden = (up + 1.0) * gate * (1.0 / (1.0 + jnp.exp(-1.702 * gate)))
            h_buf[k] = hidden.astype(bf16)
            return carry

        lax.fori_loop(0, 2, units_of, 0)
        for start in range(0, width, 768):
            size = min(768, width - start)
            cols = pl.ds(start, size)
            total = jnp.dot(h_buf[0, :, :units], raw_out[0, :, cols], preferred_element_type=f32)
            total += jnp.dot(h_buf[1, :, :units], raw_out[1, :, cols], preferred_element_type=f32)
            own_part[c, :, cols] = total[:rows]
            part_send[pl.ds(c * per, per), :, cols] = total[rows:].astype(bf16).reshape(per, capacity, size)

    def give_back(c):
        wait_sent(out_buf, go_send, c)
        total = own_part[c] + part_recv[pl.ds(c * per, per)].astype(f32).reshape(rows, width)
        out_buf[pl.ds(c * per, per)] = total.astype(bf16).reshape(per, capacity, width)

        def one(m, carry):
            index = c * per + m
            remote(
                out_buf.at[index], ret_recv.at[index], ret_send.at[c], ret_rsem.at[c], (x, peer(e, index, -1, cores, ys, zs))
            ).start()
            return carry

        lax.fori_loop(jnp.where(c == 0, 1, 0), per, one, 0)

    def step(t, carry):
        @pl.when(t < 4)
        def _():
            wait_own(t)
            forward(t).start()

        @pl.when(t == 1)
        def _():
            weight_in.wait()
            separate(1)
            weight_out.wait()

        @pl.when((t >= 1) & (t < 5))
        def _():
            forward(t - 1).wait_recv()
            compute(t - 1)
            partial(t - 1).start()

        @pl.when(t >= 2)
        def _():
            partial(t - 2).wait_recv()
            give_back(t - 2)

        return carry

    lax.fori_loop(0, 6, step, 0)
    ret_recv[0] = out_buf[0]

    def finish(c, carry):
        forward(c).wait_send()
        partial(c).wait_send()
        wait_sent(out_buf, ret_send, c)

        @pl.when(c == 0)
        def _():
            view = ret_recv.at[pl.ds(1, per - 1)]
            remote(view, view, go_send.at[0], ret_rsem.at[0], twin).wait_recv()

        @pl.when(c > 0)
        def _():
            view = chunk_of(ret_recv, c)
            remote(view, view, go_send.at[0], ret_rsem.at[c], twin).wait_recv()

        return carry

    lax.fori_loop(0, 4, finish, 0)
    for start in range(0, width, 768):
        size = min(768, width - start)
        cols = pl.ds(start, size)
        back = ret_recv[:, :, cols].reshape(slabs * capacity, size)
        mixed = jnp.dot(combine[0], back, preferred_element_type=f32)
        mixed += jnp.dot(combine[1], back, preferred_element_type=f32)
        result[:, cols] = (residual[:, cols] + mixed).astype(bf16)


def experts(grid, dispatch, normed, residual, combine, own_in, near_in, own_out):
    slots, row_count = dispatch.shape
    width = normed.shape[1]
    columns = own_in.shape[0]
    units = columns // 2
    padded = -(-units // 128) * 128
    slabs = grid[0] * grid[1] * grid[2]
    capacity = slots // slabs
    rows = slots // 4
    vmem = pl.BlockSpec(memory_space=pltpu.VMEM)
    hbm = pl.BlockSpec(memory_space=pl.ANY)
    dma = pltpu.SemaphoreType.DMA
    buffer = pltpu.VMEM((slabs, capacity, width), bf16)
    return pl.pallas_call(
        functools.partial(expert_kernel, grid),
        out_shape=jax.ShapeDtypeStruct((row_count, width), bf16),
        in_specs=[vmem, vmem, vmem, vmem, hbm, hbm, hbm],
        out_specs=vmem,
        scratch_shapes=[
            pltpu.VMEM((2, columns, width), bf16),
            pltpu.VMEM((2, 2 * padded, width), bf16),
            pltpu.VMEM((2, units, width), bf16),
            buffer,
            buffer,
            buffer,
            pltpu.VMEM((2 * rows, width), bf16),
            pltpu.VMEM((2, 2 * rows, padded), bf16),
            pltpu.VMEM((4, rows, width), f32),
            buffer,
            buffer,
            buffer,
            dma((3,)),
            dma((2,)),
            dma((2,)),
        ]
        + [dma((4,))] * 8,
        compiler_params=pltpu.CompilerParams(collective_id=1, has_side_effects=True, vmem_limit_bytes=60 << 20),
        cost_estimate=pl.CostEstimate(flops=14 << 30, bytes_accessed=30 << 20, transcendentals=0),
        name="experts",
    )(dispatch, normed, residual, combine, own_in, near_in, own_out)


PIECE = 384
PIECES = 8


def attention_kernel(
    grid,
    destination,
    lengths,
    expert_index,
    router_weights,
    stream_t,
    query,
    key_value,
    weight_hbm,
    own_in,
    residual,
    normed,
    dispatch,
    combine,
    near_in,
    weight_t,
    shuffle,
    stack,
    early_out,
    early_in,
    late_out,
    late_in,
    sorted_rows,
    section,
    context,
    parts,
    columns,
    local_sem,
    near_send,
    near_recv,
    early_send,
    early_recv,
    late_send,
    late_recv,
    key_send,
    key_recv,
    context_send,
    context_recv,
    column_send,
    column_recv,
):
    cores, ys, zs = grid
    x = lax.axis_index("dp")
    e = lax.axis_index("expert")
    count = cores * ys * zs
    rows = destination.shape[1]
    share = rows // count
    width = residual.shape[1]
    slab = PIECES * share
    mesh_id = pl.DeviceIdType.MESH

    def remote(src, dst, ssem, rsem, device):
        return pltpu.make_async_remote_copy(
            src_ref=src, dst_ref=dst, send_sem=ssem, recv_sem=rsem, device_id=device, device_id_type=mesh_id
        )

    barrier = pltpu.get_barrier_semaphore()

    def greet(step, carry):
        pl.semaphore_signal(barrier, inc=1, device_id=(x, (e + step) % count), device_id_type=mesh_id)
        return carry

    lax.fori_loop(1, count, greet, 0)
    for s in range(1, 4):
        pl.semaphore_signal(barrier, inc=1, device_id=((x + s) % 4, e), device_id_type=mesh_id)
    load = pltpu.make_async_copy(weight_hbm, weight_t, local_sem)
    load.start()

    size = count * slab
    row = lax.broadcasted_iota(jnp.int32, (size, 1), 0)
    column = lax.broadcasted_iota(jnp.int32, (size, size), 1)
    source = (row % slab) // share * rows + row // slab * share + row % share
    shuffle[0] = (column == source).astype(f32).astype(bf16)
    source = (row % rows) // share * slab + row // rows * share + row % share
    shuffle[1] = (column == source).astype(f32).astype(bf16)

    def pack(values, out):
        stack[...] = jnp.zeros_like(stack)
        for start, value in values:
            done = 0
            while done < value.shape[1]:
                piece, offset = (start + done) // PIECE, (start + done) % PIECE
                part = min(PIECE - offset, value.shape[1] - done)
                stack[pl.ds(piece * rows, rows), pl.ds(offset, part)] = value[:, done : done + part]
                done += part
        out[...] = (
            jnp.dot(shuffle[0], stack[...], preferred_element_type=f32).astype(bf16).reshape(count, slab, PIECE)
        )

    def unpack(got):
        stack[...] = jnp.dot(
            shuffle[1], got[...].reshape(size, PIECE), preferred_element_type=f32
        ).astype(bf16)

    def send_all(src, dst, ssem, rsem):
        def one(index, carry):
            remote(src.at[index], dst.at[index], ssem, rsem, (x, peer(e, index, 1, cores, ys, zs))).start()
            return carry

        lax.fori_loop(1, count, one, 0)
        dst[0] = src[0]

    def all_of(src, dst, ssem, rsem):
        return remote(src.at[pl.ds(1, count - 1)], dst.at[pl.ds(1, count - 1)], ssem, rsem, (x, (e + 1) % count))

    across = lax.broadcasted_iota(jnp.int32, (rows, rows), 1)
    down = lax.broadcasted_iota(jnp.int32, (rows, rows), 0)
    target_row = jnp.broadcast_to(destination[...], (rows, rows))
    target_col = jnp.sum(jnp.where(across == down, target_row, 0), axis=1, keepdims=True)
    bits = (4 * rows).bit_length() - 1
    pack_row = lax.shift_right_logical(target_row, bits)
    pack_col = lax.shift_right_logical(target_col, bits)
    rank = jnp.sum(((pack_row == pack_col) & (down < across)).astype(jnp.int32), axis=0, keepdims=True)
    index = lax.broadcasted_iota(jnp.int32, (rows, 1), 0)
    slot = peer(e, index // share, 1, cores, ys, zs) * share + index % share
    sender = (slot == pack_row * share + rank).astype(f32).astype(bf16)
    lane = lax.broadcasted_iota(jnp.int32, (rows, 128), 1)
    place = (lane == (target_col & (rows - 1))).astype(f32).astype(bf16)

    query_width, memory_width = query.shape[1], key_value.shape[1]
    early_width = query_width + memory_width
    pack(
        [
            (0, jnp.dot(sender, query[...], preferred_element_type=f32).astype(bf16)),
            (query_width, jnp.dot(sender, key_value[...], preferred_element_type=f32).astype(bf16)),
            (early_width, jnp.dot(sender, place, preferred_element_type=f32).astype(bf16)),
        ],
        early_out,
    )
    pl.semaphore_wait(barrier, count + 2)
    near = remote(
        own_in.at[pl.ds(0, near_in.shape[0])], near_in, near_send, near_recv, (weight_pair(x, e % cores), e)
    )
    near.start()
    send_all(early_out, early_in, early_send, early_recv)
    pack(
        [
            (
                0,
                lax.dot_general(
                    sender, stream_t[...], (((1,), (1,)), ((), ())), preferred_element_type=f32
                ).astype(bf16),
            )
        ],
        late_out,
    )
    send_all(late_out, late_in, late_send, late_recv)

    slots, capacity = dispatch.shape[0], dispatch.shape[0] // count
    holder = peer(e, lax.broadcasted_iota(jnp.int32, (count, 1), 0), 1, cores, ys, zs)
    chosen = jnp.zeros((count, rows), f32)
    weight = jnp.zeros((count, rows), f32)
    for k in range(TOPK):
        match = holder == expert_index[k : k + 1, :]
        chosen += match.astype(f32)
        weight += jnp.where(match, router_weights[k : k + 1, :], 0.0)
    before = (down < across).astype(f32).astype(bf16)
    earlier = jnp.dot(chosen.astype(bf16), before, preferred_element_type=f32)
    earlier = jnp.where(chosen > 0.0, earlier, -1.0)
    slot_row = lax.broadcasted_iota(jnp.int32, (slots, count), 0)
    spread = (slot_row // capacity == lax.broadcasted_iota(jnp.int32, (slots, count), 1)).astype(f32).astype(bf16)
    number = (lax.broadcasted_iota(jnp.int32, (slots, rows), 0) % capacity).astype(f32)
    taken = jnp.dot(spread, earlier.astype(bf16), preferred_element_type=f32) == number
    dispatch[...] = taken.astype(f32).astype(bf16)
    high = weight.astype(bf16)
    low = (weight - high.astype(f32)).astype(bf16)
    for i, value in enumerate((high, low)):
        wide = jnp.dot(spread, value, preferred_element_type=f32)
        combine[i] = jnp.transpose(jnp.where(taken, wide, 0.0)).astype(bf16)

    all_of(early_out, early_in, early_send, early_recv).wait_recv()
    unpack(early_in)
    last, offset = early_width // PIECE, early_width % PIECE
    spots = stack[pl.ds(last * rows, rows), pl.ds(offset, 128)].astype(f32)
    settle = jnp.transpose(spots)[:rows].astype(bf16)
    for piece in range(last + 1):
        part = min(PIECE, early_width - piece * PIECE)
        moved = jnp.dot(settle, stack[pl.ds(piece * rows, rows), :], preferred_element_type=f32).astype(bf16)
        sorted_rows[:, pl.ds(piece * PIECE, part)] = moved[:, :part]
    section[0] = sorted_rows[:, pl.ds(query_width, memory_width)]
    for s in range(1, 4):
        remote(section.at[0], section.at[s], key_send, key_recv, ((x + s) % 4, e)).start()

    keys = remote(section.at[pl.ds(1, 3)], section.at[pl.ds(1, 3)], key_send, key_recv, ((x + 1) % 4, e))
    keys.wait_recv()
    key_count = 4 * rows
    group = HEADS // KV_HEADS
    key_width = KV_HEADS * HEAD_DIM
    first, second = lengths[0, 0], lengths[0, 0] + lengths[0, 1]

    def segment(position):
        return (position >= first).astype(jnp.int32) + (position >= second).astype(jnp.int32)

    key_lane = lax.broadcasted_iota(jnp.int32, (rows, key_count), 1)
    key_place = (x + 4 - key_lane // rows) % 4 * rows + key_lane % rows
    query_place = x * rows + lax.broadcasted_iota(jnp.int32, (rows, key_count), 0)
    seen = ((segment(key_place) == segment(query_place)) & (key_place <= query_place))[None]
    for h in range(KV_HEADS):
        key = section[:, :, h * HEAD_DIM : (h + 1) * HEAD_DIM].reshape(key_count, HEAD_DIM)
        value = section[:, :, key_width + h * HEAD_DIM : key_width + (h + 1) * HEAD_DIM].reshape(
            key_count, HEAD_DIM
        )
        head_rows = jnp.concatenate(
            [
                sorted_rows[:, (h * group + g) * HEAD_DIM : (h * group + g + 1) * HEAD_DIM]
                for g in range(group)
            ],
            axis=0,
        )
        scores = lax.dot_general(
            head_rows, key, (((1,), (1,)), ((), ())), preferred_element_type=f32
        ) * HEAD_DIM ** (-0.5)
        scores = jnp.where(seen, scores.reshape(group, rows, key_count), masked_score)
        top = jnp.max(scores, axis=-1, keepdims=True)
        weights = jnp.where(seen, jnp.exp(scores - top), 0.0)
        denominator = jnp.sum(weights, axis=-1, keepdims=True)
        numerator = jnp.dot(
            weights.astype(bf16).reshape(group * rows, key_count), value, preferred_element_type=f32
        ).reshape(group, rows, HEAD_DIM)
        heads = (numerator / denominator).astype(bf16)
        context[0, h] = jnp.concatenate([heads[g] for g in range(group)], axis=1)
        for s in (2, 1, 3):
            remote(
                context.at[0, h], context.at[s, h], context_send.at[s - 1], context_recv.at[s - 1], ((x + s) % 4, e)
            ).start()

    load.wait()
    depth = group * HEAD_DIM

    def project(s):
        total = None
        for h in range(KV_HEADS):
            term = lax.dot_general(
                context[s, h],
                weight_t[:, pl.ds(h * depth, depth)],
                (((1,), (1,)), ((), ())),
                preferred_element_type=f32,
            )
            total = term if total is None else total + term
        return total.astype(bf16)

    def whole_context(s):
        return remote(
            context.at[0], context.at[s], context_send.at[s - 1], context_recv.at[s - 1], ((x + s) % 4, e)
        )

    columns[x] = project(0)
    all_of(late_out, late_in, late_send, late_recv).wait_recv()
    unpack(late_in)
    for start in range(0, width, PIECE):
        part = min(PIECE, width - start)
        moved = jnp.dot(
            settle, stack[pl.ds(start // PIECE * rows, rows), :], preferred_element_type=f32
        )
        residual[:, pl.ds(start, part)] = moved[:, :part]
    for s in (1, 3, 2):
        whole_context(s).wait_recv()
        parts[s - 1] = project(s)
        remote(parts.at[s - 1], columns.at[x], column_send, column_recv, ((x + 4 - s) % 4, e)).start()
    done = remote(parts, columns.at[pl.ds(0, 3)], column_send, column_recv, ((x + 1) % 4, e))
    done.wait_recv()
    update = jnp.concatenate([columns[d] for d in range(4)], axis=1).astype(f32)
    total = residual[...] + update
    residual[...] = total
    scale = lax.rsqrt(jnp.mean(total * total, axis=-1, keepdims=True) + norm_eps)
    normed[...] = (total * scale).astype(bf16)
    done.wait_send()
    near.wait()
    keys.wait_send()
    for s in range(1, 4):
        whole_context(s).wait_send()
    all_of(early_out, early_in, early_send, early_recv).wait_send()
    all_of(late_out, late_in, late_send, late_recv).wait_send()


def attend(grid, sent, destination, lengths, expert_index, router_weights, stream_t, query, key_value, weight_t, own_in):
    rows = destination.shape[1]
    width = stream_t.shape[0]
    count = grid[0] * grid[1] * grid[2]
    slab = PIECES * (rows // count)
    size = count * slab
    slots = rows * TOPK
    vmem = pl.BlockSpec(memory_space=pltpu.VMEM)
    hbm = pl.BlockSpec(memory_space=pl.ANY)
    dma = pltpu.SemaphoreType.DMA
    slabs = pltpu.VMEM((count, slab, PIECE), bf16)
    early_width = query.shape[1] + key_value.shape[1]
    return pl.pallas_call(
        functools.partial(attention_kernel, grid),
        out_shape=[
            jax.ShapeDtypeStruct((rows, width), f32),
            jax.ShapeDtypeStruct((rows, width), bf16),
            jax.ShapeDtypeStruct((slots, rows), bf16),
            jax.ShapeDtypeStruct((2, rows, slots), bf16),
            jax.ShapeDtypeStruct((sent, width), bf16),
        ],
        in_specs=[vmem, pl.BlockSpec(memory_space=pltpu.SMEM)] + [vmem] * 5 + [hbm] * 2,
        out_specs=[vmem] * 4 + [hbm],
        scratch_shapes=[
            pltpu.VMEM(weight_t.shape, bf16),
            pltpu.VMEM((2, size, size), bf16),
            pltpu.VMEM((size, PIECE), bf16),
            slabs,
            slabs,
            slabs,
            slabs,
            pltpu.VMEM((rows, early_width), bf16),
            pltpu.VMEM((4, rows, key_value.shape[1]), bf16),
            pltpu.VMEM((4, KV_HEADS, rows, HEADS // KV_HEADS * HEAD_DIM), bf16),
            pltpu.VMEM((3, rows, width // 4), bf16),
            pltpu.VMEM((4, rows, width // 4), bf16),
        ]
        + [dma] * 9
        + [dma((3,))] * 2
        + [dma] * 2,
        compiler_params=pltpu.CompilerParams(
            collective_id=2, has_side_effects=True, vmem_limit_bytes=60 << 20
        ),
        cost_estimate=pl.CostEstimate(flops=5 << 30, bytes_accessed=8 << 20, transcendentals=0),
        name="attend",
    )(destination, lengths, expert_index, router_weights, stream_t, query, key_value, weight_t, own_in)


def on_device(
    stream_rows,
    query_rows,
    key_value_rows,
    destination,
    lengths,
    out_weight,
    expert_index,
    router_weights,
    gate_up,
    down_weight,
):
    row_count, model_width = stream_rows.shape
    expert_count = lax.axis_size("expert")
    cores, ys = 2, 4
    grid = (cores, ys, expert_count // (cores * ys))
    own_in = gate_up[0].T
    sent = own_in.shape[0] * 5 // 128 * 16
    residual, normed, dispatch, combine, near_in = attend(
        grid,
        sent,
        destination.reshape(1, row_count),
        lengths,
        expert_index[0].T,
        router_weights[0].T,
        stream_rows.T,
        query_rows,
        key_value_rows,
        out_weight.T,
        own_in,
    )
    scored = experts(grid, dispatch, normed, residual, combine, own_in, near_in, down_weight[0])
    return scored.reshape(1, row_count, model_width)


def solution(mesh):
    placed = (
        P(("dp", "expert"), None),
        P(("dp", "expert"), None),
        P(("dp", "expert"), None),
        P(("dp", "expert")),
        P("expert", None),
        P(None, "dp"),
        P("expert", "dp", None),
        P("expert", "dp", None),
        P("expert", None, "dp"),
        P("expert", "dp", None),
    )
    return jax.shard_map(
        on_device, mesh=mesh, in_specs=placed, out_specs=P("expert", "dp", None), check_vma=False
    )
```

```python
import functools

import jax
import jax.numpy as jnp
from jax import lax
from jax.experimental import pallas as pl
from jax.experimental.pallas import tpu as pltpu
from jax.sharding import PartitionSpec as P

HEADS = 32
KV_HEADS = 4
HEAD_DIM = 64
TOPK = 4


masked_score = -1e30
norm_eps = 1e-05
f32 = jnp.float32
bf16 = jnp.bfloat16


def relation(index, cores, ys, zs):
    per = zs * cores
    half = max(zs // 2, 1)
    chunk, rest = index // per, index % per
    turn = rest // cores
    dz = (turn % 2) * (half + turn // 2) + (1 - turn % 2) * ((half - turn // 2) % half)
    return dz, (chunk + zs * ys - dz) % ys, rest % cores


def peer(expert, index, sign, cores, ys, zs):
    dz, dy, dc = relation(index, cores, ys, zs)
    z, y, c = expert // (ys * cores), (expert // cores) % ys, expert % cores
    z = (z + sign * dz + zs) % zs
    y = (y + sign * dy + ys) % ys
    c = (c + dc) % cores
    return (z * ys + y) * cores + c


def weight_pair(x, core):
    return (x + 5 - 2 * ((x + core) % 2)) % 4


def expert_kernel(
    grid,
    dispatch,
    normed,
    residual,
    combine,
    near,
    weight_in,
    weight_out,
    load_out,
    own_in,
    result,
    raw_in,
    split,
    raw_out,
    out_buf,
    in_own,
    in_twin,
    x_buf,
    h_buf,
    own_part,
    part_recv,
    ret_recv,
    own_sem,
    go_send,
    go_recv,
    twin_send,
    twin_recv,
    part_ssem,
    part_rsem,
    ret_send,
    ret_rsem,
):
    cores, ys, zs = grid
    x = lax.axis_index("dp")
    e = lax.axis_index("expert")
    twin = (weight_pair(x, 1 - e % cores), e)
    slabs, capacity, width = out_buf.shape
    per = slabs // 4
    rows = per * capacity
    columns = raw_in.shape[1]
    units = columns // 2
    padded = split.shape[0] // 4

    def remote(src, dst, ssem, rsem, device):
        return pltpu.make_async_remote_copy(
            src_ref=src, dst_ref=dst, send_sem=ssem, recv_sem=rsem, device_id=device, device_id_type=pl.DeviceIdType.MESH
        )

    load_own = pltpu.make_async_copy(own_in, raw_in.at[0], own_sem)
    load_own.start()

    def chunk_of(ref, c):
        return ref.at[pl.ds(c * per, per)]

    def pack_dispatch(c):
        picked = jnp.dot(dispatch[pl.ds(c * rows, rows), :], normed[...], preferred_element_type=f32)
        out_buf[pl.ds(c * per, per)] = picked.astype(bf16).reshape(per, capacity, width)

    def send_dispatch(c):
        def one(m, carry):
            index = c * per + m
            remote(
                out_buf.at[index], in_own.at[index], go_send.at[c], go_recv.at[c], (x, peer(e, index, 1, cores, ys, zs))
            ).start()
            return carry

        lax.fori_loop(jnp.where(c == 0, 1, 0), per, one, 0)

    def begin(c, carry):
        pack_dispatch(c)
        send_dispatch(c)
        return carry

    lax.fori_loop(0, 4, begin, 0)
    in_own[0] = out_buf[0]

    row = lax.broadcasted_iota(jnp.int32, (2 * padded, columns), 0)
    column = lax.broadcasted_iota(jnp.int32, (2 * padded, columns), 1)
    unit = jnp.where(row < padded, row, row - padded)
    wanted = jnp.where(unit < units, 2 * unit + jnp.where(row < padded, 0, 1), -1)
    part = (column == wanted).astype(f32).astype(bf16)

    def separate(k):
        for start in range(0, width, 768):
            cols = pl.ds(start, min(768, width - start))
            split[pl.ds(k * 2 * padded, 2 * padded), cols] = jnp.dot(part, raw_in[k, :, cols], preferred_element_type=f32).astype(bf16)

    load_own.wait()
    separate(0)
    load_out.wait()
    near.wait()

    def wait_own(c):
        @pl.when(c == 0)
        def _():
            view = in_own.at[pl.ds(1, per - 1)]
            remote(view, view, go_send.at[0], go_recv.at[0], twin).wait_recv()

        @pl.when(c > 0)
        def _():
            view = chunk_of(in_own, c)
            remote(view, view, go_send.at[c], go_recv.at[c], twin).wait_recv()

    def forward(c):
        return remote(chunk_of(in_own, c), chunk_of(in_twin, c), twin_send.at[c], twin_recv.at[c], twin)

    def partial(c):
        return remote(chunk_of(in_twin, c), chunk_of(part_recv, c), part_ssem.at[c], part_rsem.at[c], twin)

    def wait_sent(ref, sems, c):
        @pl.when(c == 0)
        def _():
            view = ref.at[pl.ds(1, per - 1)]
            remote(view, view, sems.at[0], go_recv.at[0], twin).wait_send()

        @pl.when(c > 0)
        def _():
            view = chunk_of(ref, c)
            remote(view, view, sems.at[c], go_recv.at[c], twin).wait_send()

    def compute(c):
        x_buf[pl.ds(0, rows), :] = in_own[pl.ds(c * per, per)].reshape(rows, width)
        x_buf[pl.ds(rows, rows), :] = in_twin[pl.ds(c * per, per)].reshape(rows, width)

        def units_of(k, carry):
            projected = lax.dot_general(
                x_buf[...],
                split[pl.ds(pl.multiple_of(k * 2 * padded, 128), 2 * padded), :],
                (((1,), (1,)), ((), ())), preferred_element_type=f32
            )
            gate = projected[:, :padded]
            up = projected[:, padded:]
            hidden = (up + 1.0) * gate * (1.0 / (1.0 + jnp.exp(-1.702 * gate)))
            h_buf[k] = hidden.astype(bf16)
            return carry

        lax.fori_loop(0, 2, units_of, 0)
        for start in range(0, width, 768):
            size = min(768, width - start)
            cols = pl.ds(start, size)
            total = jnp.dot(h_buf[0, :, :units], raw_out[0, :, cols], preferred_element_type=f32)
            total += jnp.dot(h_buf[1, :, :units], raw_out[1, :, cols], preferred_element_type=f32)
            own_part[c % 2, :, cols] = total[:rows]
            in_twin[pl.ds(c * per, per), :, cols] = total[rows:].astype(bf16).reshape(per, capacity, size)

    def give_back(c):
        wait_sent(out_buf, go_send, c)
        total = own_part[c % 2] + part_recv[pl.ds(c * per, per)].astype(f32).reshape(rows, width)
        out_buf[pl.ds(c * per, per)] = total.astype(bf16).reshape(per, capacity, width)

        def one(m, carry):
            index = c * per + m
            remote(
                out_buf.at[index], ret_recv.at[index], ret_send.at[c], ret_rsem.at[c], (x, peer(e, index, -1, cores, ys, zs))
            ).start()
            return carry

        lax.fori_loop(jnp.where(c == 0, 1, 0), per, one, 0)

    def step(t, carry):
        @pl.when(t < 4)
        def _():
            wait_own(t)
            forward(t).start()

        @pl.when(t == 1)
        def _():
            weight_in.wait()
            separate(1)
            weight_out.wait()

        @pl.when((t >= 1) & (t < 5))
        def _():
            forward(t - 1).wait_recv()
            compute(t - 1)
            partial(t - 1).start()

        @pl.when(t >= 2)
        def _():
            partial(t - 2).wait_recv()
            give_back(t - 2)

        return carry

    lax.fori_loop(0, 6, step, 0)
    ret_recv[0] = out_buf[0]

    def finish(c, carry):
        forward(c).wait_send()
        partial(c).wait_send()
        wait_sent(out_buf, ret_send, c)

        @pl.when(c == 0)
        def _():
            view = ret_recv.at[pl.ds(1, per - 1)]
            remote(view, view, go_send.at[0], ret_rsem.at[0], twin).wait_recv()

        @pl.when(c > 0)
        def _():
            view = chunk_of(ret_recv, c)
            remote(view, view, go_send.at[0], ret_rsem.at[c], twin).wait_recv()

        return carry

    lax.fori_loop(0, 4, finish, 0)
    for start in range(0, width, 768):
        size = min(768, width - start)
        cols = pl.ds(start, size)
        back = ret_recv[:, :, cols].reshape(slabs * capacity, size)
        mixed = jnp.dot(combine[0], back, preferred_element_type=f32)
        mixed += jnp.dot(combine[1], back, preferred_element_type=f32)
        result[:, cols] = (residual[:, cols] + mixed).astype(bf16)


PIECE = 384
PIECES = 8


def attention_kernel(
    grid,
    destination,
    lengths,
    expert_index,
    router_weights,
    stream_t,
    query,
    key_value,
    weight_hbm,
    near,
    weight_rest,
    residual,
    normed,
    dispatch,
    combine,
    weight_t,
    shuffle,
    stack,
    early_out,
    early_in,
    late_out,
    late_in,
    sorted_rows,
    section,
    context,
    parts,
    columns,
    local_sem,
    early_send,
    early_recv,
    late_send,
    late_recv,
    key_send,
    key_recv,
    context_send,
    context_recv,
    column_send,
    column_recv,
):
    cores, ys, zs = grid
    x = lax.axis_index("dp")
    e = lax.axis_index("expert")
    count = cores * ys * zs
    rows = destination.shape[1]
    share = rows // count
    width = residual.shape[1]
    slab = PIECES * share
    mesh_id = pl.DeviceIdType.MESH

    def remote(src, dst, ssem, rsem, device):
        return pltpu.make_async_remote_copy(
            src_ref=src, dst_ref=dst, send_sem=ssem, recv_sem=rsem, device_id=device, device_id_type=mesh_id
        )

    barrier = pltpu.get_barrier_semaphore()

    def greet(step, carry):
        pl.semaphore_signal(barrier, inc=1, device_id=(x, (e + step) % count), device_id_type=mesh_id)
        return carry

    lax.fori_loop(1, count, greet, 0)
    for s in range(1, 4):
        pl.semaphore_signal(barrier, inc=1, device_id=((x + s) % 4, e), device_id_type=mesh_id)
    load = pltpu.make_async_copy(weight_hbm, weight_t, local_sem)
    load.start()

    size = count * slab
    row = lax.broadcasted_iota(jnp.int32, (size, 1), 0)
    column = lax.broadcasted_iota(jnp.int32, (size, size), 1)
    source = (row % slab) // share * rows + row // slab * share + row % share
    shuffle[0][...] = (column == source).astype(f32).astype(bf16)
    source = (row % rows) // share * slab + row // rows * share + row % share
    shuffle[1][...] = (column == source).astype(f32).astype(bf16)

    def pack(values, out):
        stack[...] = jnp.zeros_like(stack)
        for start, value in values:
            done = 0
            while done < value.shape[1]:
                piece, offset = (start + done) // PIECE, (start + done) % PIECE
                part = min(PIECE - offset, value.shape[1] - done)
                stack[pl.ds(piece * rows, rows), pl.ds(offset, part)] = value[:, done : done + part]
                done += part
        out[...] = (
            jnp.dot(shuffle[0][...], stack[...], preferred_element_type=f32).astype(bf16).reshape(count, slab, PIECE)
        )

    def unpack(got):
        stack[...] = jnp.dot(
            shuffle[1][...], got[...].reshape(size, PIECE), preferred_element_type=f32
        ).astype(bf16)

    def send_all(src, dst, ssem, rsem):
        def one(index, carry):
            remote(src.at[index], dst.at[index], ssem, rsem, (x, peer(e, index, 1, cores, ys, zs))).start()
            return carry

        lax.fori_loop(1, count, one, 0)
        dst[0] = src[0]

    def all_of(src, dst, ssem, rsem):
        return remote(src.at[pl.ds(1, count - 1)], dst.at[pl.ds(1, count - 1)], ssem, rsem, (x, (e + 1) % count))

    across = lax.broadcasted_iota(jnp.int32, (rows, rows), 1)
    down = lax.broadcasted_iota(jnp.int32, (rows, rows), 0)
    target_row = jnp.broadcast_to(destination[...], (rows, rows))
    target_col = jnp.sum(jnp.where(across == down, target_row, 0), axis=1, keepdims=True)
    bits = (4 * rows).bit_length() - 1
    pack_row = lax.shift_right_logical(target_row, bits)
    pack_col = lax.shift_right_logical(target_col, bits)
    rank = jnp.sum(((pack_row == pack_col) & (down < across)).astype(jnp.int32), axis=0, keepdims=True)
    index = lax.broadcasted_iota(jnp.int32, (rows, 1), 0)
    slot = peer(e, index // share, 1, cores, ys, zs) * share + index % share
    sender = (slot == pack_row * share + rank).astype(f32).astype(bf16)
    lane = lax.broadcasted_iota(jnp.int32, (rows, 128), 1)
    place = (lane == (target_col & (rows - 1))).astype(f32).astype(bf16)

    query_width, memory_width = query.shape[1], key_value.shape[1]
    early_width = query_width + memory_width
    pack(
        [
            (0, jnp.dot(sender, query[...], preferred_element_type=f32).astype(bf16)),
            (query_width, jnp.dot(sender, key_value[...], preferred_element_type=f32).astype(bf16)),
            (early_width, jnp.dot(sender, place, preferred_element_type=f32).astype(bf16)),
        ],
        early_out,
    )
    pl.semaphore_wait(barrier, count + 2)
    near.start()
    send_all(early_out, early_in, early_send, early_recv)
    pack(
        [
            (
                0,
                lax.dot_general(
                    sender, stream_t[...], (((1,), (1,)), ((), ())), preferred_element_type=f32
                ).astype(bf16),
            )
        ],
        late_out,
    )
    send_all(late_out, late_in, late_send, late_recv)

    slots, capacity = dispatch.shape[0], dispatch.shape[0] // count
    holder = peer(e, lax.broadcasted_iota(jnp.int32, (count, 1), 0), 1, cores, ys, zs)
    chosen = jnp.zeros((count, rows), f32)
    weight = jnp.zeros((count, rows), f32)
    for k in range(TOPK):
        match = holder == expert_index[k : k + 1, :]
        chosen += match.astype(f32)
        weight += jnp.where(match, router_weights[k : k + 1, :], 0.0)
    before = (down < across).astype(f32).astype(bf16)
    earlier = jnp.dot(chosen.astype(bf16), before, preferred_element_type=f32)
    earlier = jnp.where(chosen > 0.0, earlier, -1.0)
    slot_row = lax.broadcasted_iota(jnp.int32, (slots, count), 0)
    spread = (slot_row // capacity == lax.broadcasted_iota(jnp.int32, (slots, count), 1)).astype(f32).astype(bf16)
    number = (lax.broadcasted_iota(jnp.int32, (slots, rows), 0) % capacity).astype(f32)
    taken = jnp.dot(spread, earlier.astype(bf16), preferred_element_type=f32) == number
    dispatch[...] = taken.astype(f32).astype(bf16)
    high = weight.astype(bf16)
    low = (weight - high.astype(f32)).astype(bf16)
    for i, value in enumerate((high, low)):
        wide = jnp.dot(spread, value, preferred_element_type=f32)
        combine[i] = jnp.transpose(jnp.where(taken, wide, 0.0)).astype(bf16)

    all_of(early_out, early_in, early_send, early_recv).wait_recv()
    unpack(early_in)
    last, offset = early_width // PIECE, early_width % PIECE
    spots = stack[pl.ds(last * rows, rows), pl.ds(offset, 128)].astype(f32)
    settle = jnp.transpose(spots)[:rows].astype(bf16)
    for piece in range(last + 1):
        part = min(PIECE, early_width - piece * PIECE)
        moved = jnp.dot(settle, stack[pl.ds(piece * rows, rows), :], preferred_element_type=f32).astype(bf16)
        sorted_rows[:, pl.ds(piece * PIECE, part)] = moved[:, :part]
    section[0] = sorted_rows[:, pl.ds(query_width, memory_width)]
    for s in range(1, 4):
        remote(section.at[0], section.at[s], key_send, key_recv, ((x + s) % 4, e)).start()

    keys = remote(section.at[pl.ds(1, 3)], section.at[pl.ds(1, 3)], key_send, key_recv, ((x + 1) % 4, e))
    keys.wait_recv()
    key_count = 4 * rows
    group = HEADS // KV_HEADS
    key_width = KV_HEADS * HEAD_DIM
    first, second = lengths[0, 0], lengths[0, 0] + lengths[0, 1]

    def segment(position):
        return (position >= first).astype(jnp.int32) + (position >= second).astype(jnp.int32)

    key_lane = lax.broadcasted_iota(jnp.int32, (rows, key_count), 1)
    key_place = (x + 4 - key_lane // rows) % 4 * rows + key_lane % rows
    query_place = x * rows + lax.broadcasted_iota(jnp.int32, (rows, key_count), 0)
    seen = ((segment(key_place) == segment(query_place)) & (key_place <= query_place))[None]
    for h in range(KV_HEADS):
        key = section[:, :, h * HEAD_DIM : (h + 1) * HEAD_DIM].reshape(key_count, HEAD_DIM)
        value = section[:, :, key_width + h * HEAD_DIM : key_width + (h + 1) * HEAD_DIM].reshape(
            key_count, HEAD_DIM
        )
        head_rows = jnp.concatenate(
            [
                sorted_rows[:, (h * group + g) * HEAD_DIM : (h * group + g + 1) * HEAD_DIM]
                for g in range(group)
            ],
            axis=0,
        )
        scores = lax.dot_general(
            head_rows, key, (((1,), (1,)), ((), ())), preferred_element_type=f32
        ) * HEAD_DIM ** (-0.5)
        scores = jnp.where(seen, scores.reshape(group, rows, key_count), masked_score)
        top = jnp.max(scores, axis=-1, keepdims=True)
        weights = jnp.where(seen, jnp.exp(scores - top), 0.0)
        denominator = jnp.sum(weights, axis=-1, keepdims=True)
        numerator = jnp.dot(
            weights.astype(bf16).reshape(group * rows, key_count), value, preferred_element_type=f32
        ).reshape(group, rows, HEAD_DIM)
        heads = (numerator / denominator).astype(bf16)
        context[0, h] = jnp.concatenate([heads[g] for g in range(group)], axis=1)
        for s in (2, 1, 3):
            remote(
                context.at[0, h], context.at[s, h], context_send.at[s - 1], context_recv.at[s - 1], ((x + s) % 4, e)
            ).start()

    load.wait()
    depth = group * HEAD_DIM

    def project(s):
        total = None
        for h in range(KV_HEADS):
            term = lax.dot_general(
                context[s, h],
                weight_t[:, pl.ds(h * depth, depth)],
                (((1,), (1,)), ((), ())),
                preferred_element_type=f32,
            )
            total = term if total is None else total + term
        return total.astype(bf16)

    def whole_context(s):
        return remote(
            context.at[0], context.at[s], context_send.at[s - 1], context_recv.at[s - 1], ((x + s) % 4, e)
        )

    columns[x] = project(0)
    all_of(late_out, late_in, late_send, late_recv).wait_recv()
    unpack(late_in)
    for start in range(0, width, PIECE):
        part = min(PIECE, width - start)
        moved = jnp.dot(
            settle, stack[pl.ds(start // PIECE * rows, rows), :], preferred_element_type=f32
        )
        residual[:, pl.ds(start, part)] = moved[:, :part]
    for s in (1, 3, 2):
        whole_context(s).wait_recv()
        parts[s - 1] = project(s)
        remote(parts.at[s - 1], columns.at[x], column_send, column_recv, ((x + 4 - s) % 4, e)).start()
    weight_rest()
    done = remote(parts, columns.at[pl.ds(0, 3)], column_send, column_recv, ((x + 1) % 4, e))
    done.wait_recv()
    update = jnp.concatenate([columns[d] for d in range(4)], axis=1).astype(f32)
    total = residual[...] + update
    residual[...] = total
    scale = lax.rsqrt(jnp.mean(total * total, axis=-1, keepdims=True) + norm_eps)
    normed[...] = (total * scale).astype(bf16)
    done.wait_send()
    keys.wait_send()
    for s in range(1, 4):
        whole_context(s).wait_send()
    all_of(early_out, early_in, early_send, early_recv).wait_send()
    all_of(late_out, late_in, late_send, late_recv).wait_send()


def layer_kernel(
    grid,
    sent,
    destination,
    lengths,
    expert_index,
    router_weights,
    stream_t,
    query,
    key_value,
    weight_hbm,
    own_in,
    own_out,
    result,
    residual,
    normed,
    dispatch,
    combine,
    raw_in,
    split,
    raw_out,
    *rest,
):
    buffers, (weight_sem, out_sem, own_sem, pair_send, pair_recv), sems = rest[:18], rest[18:23], rest[23:]
    cores = grid[0]
    x = lax.axis_index("dp")
    e = lax.axis_index("expert")
    pair = (weight_pair(x, e % cores), e)
    columns = raw_in.shape[1]
    late_rows = pl.ds(sent, columns - sent)

    def to_pair(src, dst, i):
        return pltpu.make_async_remote_copy(
            src_ref=src,
            dst_ref=dst,
            send_sem=pair_send.at[i],
            recv_sem=pair_recv.at[i],
            device_id=pair,
            device_id_type=pl.DeviceIdType.MESH,
        )

    near = to_pair(own_in.at[pl.ds(0, sent)], raw_in.at[1, pl.ds(0, sent)], 0)
    weight_in = to_pair(own_in.at[late_rows], raw_in.at[1, late_rows], 1)
    weight_out = to_pair(own_out, raw_out.at[1], 2)
    load_out = pltpu.make_async_copy(own_out, raw_out.at[0], out_sem)
    load_out.start()

    def weight_rest():
        weight_in.start()
        weight_out.start()

    size = buffers[0].shape[0] * buffers[0].shape[1]
    height, depth = weight_hbm.shape
    if height <= columns and depth <= raw_in.shape[2]:
        weight_t = raw_in.at[0, pl.ds(0, height), pl.ds(0, depth)]
    else:
        weight_t = buffers[17]
    shuffle = [split.at[pl.ds(0, size), pl.ds(i * size, size)] for i in range(2)]
    stack = split.at[pl.ds(0, size), pl.ds(2 * size, PIECE)]
    attention_kernel(
        grid,
        destination,
        lengths,
        expert_index,
        router_weights,
        stream_t,
        query,
        key_value,
        weight_hbm,
        near,
        weight_rest,
        residual,
        normed,
        dispatch,
        combine,
        weight_t,
        shuffle,
        stack,
        *buffers[:9],
        weight_sem,
        *sems[:10],
    )
    expert_kernel(
        grid,
        dispatch,
        normed,
        residual,
        combine,
        near,
        weight_in,
        weight_out,
        load_out,
        own_in,
        result,
        raw_in,
        split,
        raw_out,
        *buffers[9:17],
        own_sem,
        *sems[10:],
    )


def layer(grid, destination, lengths, expert_index, router_weights, stream_t, query, key_value, weight_t, own_in, own_out):
    rows = destination.shape[1]
    width = stream_t.shape[0]
    count = grid[0] * grid[1] * grid[2]
    slab = PIECES * (rows // count)
    slots = rows * TOPK
    capacity = slots // count
    part = slots // 4
    columns = own_in.shape[0]
    units = columns // 2
    padded = -(-units // 128) * 128
    vmem = pl.BlockSpec(memory_space=pltpu.VMEM)
    hbm = pl.BlockSpec(memory_space=pl.ANY)
    dma = pltpu.SemaphoreType.DMA
    slabs = pltpu.VMEM((count, slab, PIECE), bf16)
    buffer = pltpu.VMEM((count, capacity, width), bf16)
    early_width = query.shape[1] + key_value.shape[1]
    carved = weight_t.shape[0] <= columns and weight_t.shape[1] <= width
    return pl.pallas_call(
        functools.partial(layer_kernel, grid, max(columns // 32, 1) * 16),
        out_shape=jax.ShapeDtypeStruct((rows, width), bf16),
        in_specs=[vmem, pl.BlockSpec(memory_space=pltpu.SMEM)] + [vmem] * 5 + [hbm] * 3,
        out_specs=vmem,
        scratch_shapes=[
            pltpu.VMEM((rows, width), f32),
            pltpu.VMEM((rows, width), bf16),
            pltpu.VMEM((slots, rows), bf16),
            pltpu.VMEM((2, rows, slots), bf16),
            pltpu.VMEM((2, columns, width), bf16),
            pltpu.VMEM((4 * padded, width), bf16),
            pltpu.VMEM((2, units, width), bf16),
            slabs,
            slabs,
            slabs,
            slabs,
            pltpu.VMEM((rows, early_width), bf16),
            pltpu.VMEM((4, rows, key_value.shape[1]), bf16),
            pltpu.VMEM((4, KV_HEADS, rows, HEADS // KV_HEADS * HEAD_DIM), bf16),
            pltpu.VMEM((3, rows, width // 4), bf16),
            pltpu.VMEM((4, rows, width // 4), bf16),
            buffer,
            buffer,
            buffer,
            pltpu.VMEM((2 * part, width), bf16),
            pltpu.VMEM((2, 2 * part, padded), bf16),
            pltpu.VMEM((2, part, width), f32),
            buffer,
            buffer,
            pltpu.VMEM((16, 128) if carved else weight_t.shape, bf16),
        ]
        + [dma, dma, dma, dma((3,)), dma((3,))]
        + [dma] * 6
        + [dma((3,))] * 2
        + [dma] * 2
        + [dma((4,))] * 8,
        compiler_params=pltpu.CompilerParams(
            collective_id=2, has_side_effects=True, vmem_limit_bytes=60 << 20
        ),
        cost_estimate=pl.CostEstimate(flops=18 << 30, bytes_accessed=30 << 20, transcendentals=0),
        name="layer",
    )(destination, lengths, expert_index, router_weights, stream_t, query, key_value, weight_t, own_in, own_out)


def on_device(
    stream_rows,
    query_rows,
    key_value_rows,
    destination,
    lengths,
    out_weight,
    expert_index,
    router_weights,
    gate_up,
    down_weight,
):
    row_count, model_width = stream_rows.shape
    expert_count = lax.axis_size("expert")
    cores, ys = 2, 4
    grid = (cores, ys, expert_count // (cores * ys))
    own_in = gate_up[0].T
    scored = layer(
        grid,
        destination.reshape(1, row_count),
        lengths,
        expert_index[0].T,
        router_weights[0].T,
        stream_rows.T,
        query_rows,
        key_value_rows,
        out_weight.T,
        own_in,
        down_weight[0],
    )
    return scored.reshape(1, row_count, model_width)


def solution(mesh):
    placed = (
        P(("dp", "expert"), None),
        P(("dp", "expert"), None),
        P(("dp", "expert"), None),
        P(("dp", "expert")),
        P("expert", None),
        P(None, "dp"),
        P("expert", "dp", None),
        P("expert", "dp", None),
        P("expert", None, "dp"),
        P("expert", "dp", None),
    )
    return jax.shard_map(
        on_device, mesh=mesh, in_specs=placed, out_specs=P("expert", "dp", None), check_vma=False
    )
```

```python
import functools

import jax
import jax.numpy as jnp
from jax import lax
from jax.experimental import pallas as pl
from jax.experimental.pallas import tpu as pltpu
from jax.sharding import PartitionSpec as P

HEADS = 32
KV_HEADS = 4
HEAD_DIM = 64
TOPK = 4


masked_score = -1e30
norm_eps = 1e-05
f32 = jnp.float32
bf16 = jnp.bfloat16


def relation(index, cores, ys, zs):
    per = zs * cores
    half = max(zs // 2, 1)
    chunk, rest = index // per, index % per
    turn = rest // cores
    dz = (turn % 2) * (half + turn // 2) + (1 - turn % 2) * ((half - turn // 2) % half)
    return dz, (chunk + zs * ys - dz) % ys, rest % cores


def peer(expert, index, sign, cores, ys, zs):
    dz, dy, dc = relation(index, cores, ys, zs)
    z, y, c = expert // (ys * cores), (expert // cores) % ys, expert % cores
    z = (z + sign * dz + zs) % zs
    y = (y + sign * dy + ys) % ys
    c = (c + dc) % cores
    return (z * ys + y) * cores + c


def weight_pair(x, core):
    return (x + 5 - 2 * ((x + core) % 2)) % 4


def expert_kernel(
    grid,
    dispatch,
    normed,
    residual,
    combine,
    near,
    weight_in,
    weight_out,
    load_out,
    own_in,
    result,
    raw_in,
    split,
    raw_out,
    out_buf,
    in_own,
    in_twin,
    x_buf,
    h_buf,
    own_part,
    part_recv,
    ret_recv,
    own_sem,
    go_send,
    go_recv,
    twin_send,
    twin_recv,
    part_ssem,
    part_rsem,
    ret_send,
    ret_rsem,
):
    cores, ys, zs = grid
    x = lax.axis_index("dp")
    e = lax.axis_index("expert")
    twin = (weight_pair(x, 1 - e % cores), e)
    slabs, capacity, width = out_buf.shape
    per = slabs // 4
    rows = per * capacity
    columns = raw_in.shape[1]
    units = columns // 2
    padded = split.shape[0] // 4

    def remote(src, dst, ssem, rsem, device):
        return pltpu.make_async_remote_copy(
            src_ref=src, dst_ref=dst, send_sem=ssem, recv_sem=rsem, device_id=device, device_id_type=pl.DeviceIdType.MESH
        )

    load_own = pltpu.make_async_copy(own_in, raw_in.at[0], own_sem)
    load_own.start()

    def chunk_of(ref, c):
        return ref.at[pl.ds(c * per, per)]

    def pack_dispatch(c):
        picked = jnp.dot(dispatch[pl.ds(c * rows, rows), :], normed[...], preferred_element_type=f32)
        out_buf[pl.ds(c * per, per)] = picked.astype(bf16).reshape(per, capacity, width)

    def send_dispatch(c):
        def one(m, carry):
            index = c * per + m
            remote(
                out_buf.at[index], in_own.at[index], go_send.at[c], go_recv.at[c], (x, peer(e, index, 1, cores, ys, zs))
            ).start()
            return carry

        lax.fori_loop(jnp.where(c == 0, 1, 0), per, one, 0)

    def begin(c, carry):
        pack_dispatch(c)
        send_dispatch(c)
        return carry

    lax.fori_loop(0, 4, begin, 0)
    in_own[0] = out_buf[0]

    row = lax.broadcasted_iota(jnp.int32, (2 * padded, columns), 0)
    column = lax.broadcasted_iota(jnp.int32, (2 * padded, columns), 1)
    unit = jnp.where(row < padded, row, row - padded)
    wanted = jnp.where(unit < units, 2 * unit + jnp.where(row < padded, 0, 1), -1)
    part = (column == wanted).astype(f32).astype(bf16)

    def separate(k):
        for start in range(0, width, 768):
            cols = pl.ds(start, min(768, width - start))
            split[pl.ds(k * 2 * padded, 2 * padded), cols] = jnp.dot(part, raw_in[k, :, cols], preferred_element_type=f32).astype(bf16)

    load_own.wait()
    separate(0)
    load_out.wait()
    near.wait()

    def wait_own(c):
        @pl.when(c == 0)
        def _():
            view = in_own.at[pl.ds(1, per - 1)]
            remote(view, view, go_send.at[0], go_recv.at[0], twin).wait_recv()

        @pl.when(c > 0)
        def _():
            view = chunk_of(in_own, c)
            remote(view, view, go_send.at[c], go_recv.at[c], twin).wait_recv()

    def forward(c):
        return remote(chunk_of(in_own, c), chunk_of(in_twin, c), twin_send.at[c], twin_recv.at[c], twin)

    def partial(c):
        return remote(chunk_of(in_twin, c), chunk_of(part_recv, c), part_ssem.at[c], part_rsem.at[c], twin)

    def wait_sent(ref, sems, c):
        @pl.when(c == 0)
        def _():
            view = ref.at[pl.ds(1, per - 1)]
            remote(view, view, sems.at[0], go_recv.at[0], twin).wait_send()

        @pl.when(c > 0)
        def _():
            view = chunk_of(ref, c)
            remote(view, view, sems.at[c], go_recv.at[c], twin).wait_send()

    def compute(c):
        x_buf[pl.ds(0, rows), :] = in_own[pl.ds(c * per, per)].reshape(rows, width)
        x_buf[pl.ds(rows, rows), :] = in_twin[pl.ds(c * per, per)].reshape(rows, width)

        def units_of(k, carry):
            projected = lax.dot_general(
                x_buf[...],
                split[pl.ds(pl.multiple_of(k * 2 * padded, 128), 2 * padded), :],
                (((1,), (1,)), ((), ())), preferred_element_type=f32
            )
            gate = projected[:, :padded]
            up = projected[:, padded:]
            hidden = (up + 1.0) * gate * (1.0 / (1.0 + jnp.exp(-1.702 * gate)))
            h_buf[k] = hidden.astype(bf16)
            return carry

        lax.fori_loop(0, 2, units_of, 0)
        for start in range(0, width, 768):
            size = min(768, width - start)
            cols = pl.ds(start, size)
            total = jnp.dot(h_buf[0, :, :units], raw_out[0, :, cols], preferred_element_type=f32)
            total += jnp.dot(h_buf[1, :, :units], raw_out[1, :, cols], preferred_element_type=f32)
            own_part[c % 2, :, cols] = total[:rows]
            in_twin[pl.ds(c * per, per), :, cols] = total[rows:].astype(bf16).reshape(per, capacity, size)

    def give_back(c):
        wait_sent(out_buf, go_send, c)
        total = own_part[c % 2] + part_recv[pl.ds(c * per, per)].astype(f32).reshape(rows, width)
        out_buf[pl.ds(c * per, per)] = total.astype(bf16).reshape(per, capacity, width)

        def one(m, carry):
            index = c * per + m
            remote(
                out_buf.at[index], ret_recv.at[index], ret_send.at[c], ret_rsem.at[c], (x, peer(e, index, -1, cores, ys, zs))
            ).start()
            return carry

        lax.fori_loop(jnp.where(c == 0, 1, 0), per, one, 0)

    def step(t, carry):
        @pl.when(t < 4)
        def _():
            wait_own(t)
            forward(t).start()

        @pl.when(t == 1)
        def _():
            weight_in.wait()
            separate(1)
            weight_out.wait()

        @pl.when((t >= 1) & (t < 5))
        def _():
            forward(t - 1).wait_recv()
            compute(t - 1)
            partial(t - 1).start()

        @pl.when(t >= 2)
        def _():
            partial(t - 2).wait_recv()
            give_back(t - 2)

        return carry

    lax.fori_loop(0, 6, step, 0)
    ret_recv[0] = out_buf[0]

    for c in range(4):
        view = ret_recv.at[pl.ds(1, per - 1)] if c == 0 else chunk_of(ret_recv, c)
        remote(view, view, go_send.at[0], ret_rsem.at[c], twin).wait_recv()
        for start in range(0, width, 768):
            size = min(768, width - start)
            cols = pl.ds(start, size)
            back = ret_recv[pl.ds(c * per, per), :, cols].reshape(rows, size)
            mixed = residual[:, cols]
            for i in range(2):
                mixed += jnp.dot(combine[i, :, pl.ds(c * rows, rows)], back, preferred_element_type=f32)
            if c < 3:
                residual[:, cols] = mixed
            else:
                result[:, cols] = mixed.astype(bf16)

    def finish(c, carry):
        forward(c).wait_send()
        partial(c).wait_send()
        wait_sent(out_buf, ret_send, c)
        return carry

    lax.fori_loop(0, 4, finish, 0)


PIECE = 384
PIECES = 8


def attention_kernel(
    grid,
    destination,
    lengths,
    expert_index,
    router_weights,
    stream_t,
    query,
    key_value,
    weight_hbm,
    near,
    weight_rest,
    residual,
    normed,
    dispatch,
    combine,
    weight_t,
    shuffle,
    stack,
    early_out,
    early_in,
    late_out,
    late_in,
    sorted_rows,
    section,
    context,
    parts,
    columns,
    local_sem,
    early_send,
    early_recv,
    late_send,
    late_recv,
    key_send,
    key_recv,
    context_send,
    context_recv,
    column_send,
    column_recv,
):
    cores, ys, zs = grid
    x = lax.axis_index("dp")
    e = lax.axis_index("expert")
    count = cores * ys * zs
    rows = destination.shape[1]
    share = rows // count
    width = residual.shape[1]
    slab = PIECES * share
    mesh_id = pl.DeviceIdType.MESH

    def remote(src, dst, ssem, rsem, device):
        return pltpu.make_async_remote_copy(
            src_ref=src, dst_ref=dst, send_sem=ssem, recv_sem=rsem, device_id=device, device_id_type=mesh_id
        )

    barrier = pltpu.get_barrier_semaphore()

    def greet(step, carry):
        pl.semaphore_signal(barrier, inc=1, device_id=(x, (e + step) % count), device_id_type=mesh_id)
        return carry

    lax.fori_loop(1, count, greet, 0)
    for s in range(1, 4):
        pl.semaphore_signal(barrier, inc=1, device_id=((x + s) % 4, e), device_id_type=mesh_id)
    load = pltpu.make_async_copy(weight_hbm, weight_t, local_sem)
    load.start()

    size = count * slab
    row = lax.broadcasted_iota(jnp.int32, (size, 1), 0)
    column = lax.broadcasted_iota(jnp.int32, (size, size), 1)
    source = (row % slab) // share * rows + row // slab * share + row % share
    shuffle[0][...] = (column == source).astype(f32).astype(bf16)

    def pack(values, out):
        stack[...] = jnp.zeros_like(stack)
        for start, value in values:
            done = 0
            while done < value.shape[1]:
                piece, offset = (start + done) // PIECE, (start + done) % PIECE
                part = min(PIECE - offset, value.shape[1] - done)
                stack[pl.ds(piece * rows, rows), pl.ds(offset, part)] = value[:, done : done + part]
                done += part
        out[...] = (
            jnp.dot(shuffle[0][...], stack[...], preferred_element_type=f32).astype(bf16).reshape(count, slab, PIECE)
        )

    def unpack(got):
        stack[...] = jnp.dot(
            shuffle[1][...], got[...].reshape(size, PIECE), preferred_element_type=f32
        ).astype(bf16)

    def send_all(src, dst, ssem, rsem):
        def one(index, carry):
            remote(src.at[index], dst.at[index], ssem, rsem, (x, peer(e, index, 1, cores, ys, zs))).start()
            return carry

        lax.fori_loop(1, count, one, 0)
        dst[0] = src[0]

    def all_of(src, dst, ssem, rsem):
        return remote(src.at[pl.ds(1, count - 1)], dst.at[pl.ds(1, count - 1)], ssem, rsem, (x, (e + 1) % count))

    across = lax.broadcasted_iota(jnp.int32, (rows, rows), 1)
    down = lax.broadcasted_iota(jnp.int32, (rows, rows), 0)
    target_row = jnp.broadcast_to(destination[...], (rows, rows))
    target_col = jnp.sum(jnp.where(across == down, target_row, 0), axis=1, keepdims=True)
    bits = (4 * rows).bit_length() - 1
    pack_row = lax.shift_right_logical(target_row, bits)
    pack_col = lax.shift_right_logical(target_col, bits)
    rank = jnp.sum(((pack_row == pack_col) & (down < across)).astype(jnp.int32), axis=0, keepdims=True)
    index = lax.broadcasted_iota(jnp.int32, (rows, 1), 0)
    slot = peer(e, index // share, 1, cores, ys, zs) * share + index % share
    sender = (slot == pack_row * share + rank).astype(f32).astype(bf16)
    lane = lax.broadcasted_iota(jnp.int32, (rows, 128), 1)
    place = (lane == (target_col & (rows - 1))).astype(f32).astype(bf16)

    query_width, memory_width = query.shape[1], key_value.shape[1]
    early_width = query_width + memory_width
    pack(
        [
            (0, jnp.dot(sender, query[...], preferred_element_type=f32).astype(bf16)),
            (query_width, jnp.dot(sender, key_value[...], preferred_element_type=f32).astype(bf16)),
            (early_width, jnp.dot(sender, place, preferred_element_type=f32).astype(bf16)),
        ],
        early_out,
    )
    pl.semaphore_wait(barrier, count + 2)
    near.start()
    send_all(early_out, early_in, early_send, early_recv)
    pack(
        [
            (
                0,
                lax.dot_general(
                    sender, stream_t[...], (((1,), (1,)), ((), ())), preferred_element_type=f32
                ).astype(bf16),
            )
        ],
        late_out,
    )
    send_all(late_out, late_in, late_send, late_recv)
    source = (row % rows) // share * slab + row // rows * share + row % share
    shuffle[1][...] = (column == source).astype(f32).astype(bf16)

    slots, capacity = dispatch.shape[0], dispatch.shape[0] // count
    holder = peer(e, lax.broadcasted_iota(jnp.int32, (count, 1), 0), 1, cores, ys, zs)
    chosen = jnp.zeros((count, rows), f32)
    weight = jnp.zeros((count, rows), f32)
    for k in range(TOPK):
        match = holder == expert_index[k : k + 1, :]
        chosen += match.astype(f32)
        weight += jnp.where(match, router_weights[k : k + 1, :], 0.0)
    before = (down < across).astype(f32).astype(bf16)
    earlier = jnp.dot(chosen.astype(bf16), before, preferred_element_type=f32)
    earlier = jnp.where(chosen > 0.0, earlier, -1.0)
    slot_row = lax.broadcasted_iota(jnp.int32, (slots, count), 0)
    spread = (slot_row // capacity == lax.broadcasted_iota(jnp.int32, (slots, count), 1)).astype(f32).astype(bf16)
    number = (lax.broadcasted_iota(jnp.int32, (slots, rows), 0) % capacity).astype(f32)
    taken = jnp.dot(spread, earlier.astype(bf16), preferred_element_type=f32) == number
    dispatch[...] = taken.astype(f32).astype(bf16)
    high = weight.astype(bf16)
    low = (weight - high.astype(f32)).astype(bf16)
    for i, value in enumerate((high, low)):
        wide = jnp.dot(spread, value, preferred_element_type=f32)
        combine[i] = jnp.transpose(jnp.where(taken, wide, 0.0)).astype(bf16)

    all_of(early_out, early_in, early_send, early_recv).wait_recv()
    unpack(early_in)
    last, offset = early_width // PIECE, early_width % PIECE
    spots = stack[pl.ds(last * rows, rows), pl.ds(offset, 128)].astype(f32)
    settle = jnp.transpose(spots)[:rows].astype(bf16)

    def move_piece(piece):
        part = min(PIECE, early_width - piece * PIECE)
        moved = jnp.dot(settle, stack[pl.ds(piece * rows, rows), :], preferred_element_type=f32).astype(bf16)
        sorted_rows[:, pl.ds(piece * PIECE, part)] = moved[:, :part]

    for piece in range(query_width // PIECE, last + 1):
        move_piece(piece)
    section[0] = sorted_rows[:, pl.ds(query_width, memory_width)]
    for s in range(1, 4):
        remote(section.at[0], section.at[s], key_send, key_recv, ((x + s) % 4, e)).start()
    for piece in range(query_width // PIECE):
        move_piece(piece)

    keys = remote(section.at[pl.ds(1, 3)], section.at[pl.ds(1, 3)], key_send, key_recv, ((x + 1) % 4, e))
    keys.wait_recv()
    key_count = 4 * rows
    group = HEADS // KV_HEADS
    key_width = KV_HEADS * HEAD_DIM
    first, second = lengths[0, 0], lengths[0, 0] + lengths[0, 1]

    def segment(position):
        return (position >= first).astype(jnp.int32) + (position >= second).astype(jnp.int32)

    key_lane = lax.broadcasted_iota(jnp.int32, (rows, key_count), 1)
    key_place = (x + 4 - key_lane // rows) % 4 * rows + key_lane % rows
    query_place = x * rows + lax.broadcasted_iota(jnp.int32, (rows, key_count), 0)
    seen = ((segment(key_place) == segment(query_place)) & (key_place <= query_place))[None]
    for h in range(KV_HEADS):
        key = section[:, :, h * HEAD_DIM : (h + 1) * HEAD_DIM].reshape(key_count, HEAD_DIM)
        value = section[:, :, key_width + h * HEAD_DIM : key_width + (h + 1) * HEAD_DIM].reshape(
            key_count, HEAD_DIM
        )
        head_rows = jnp.concatenate(
            [
                sorted_rows[:, (h * group + g) * HEAD_DIM : (h * group + g + 1) * HEAD_DIM]
                for g in range(group)
            ],
            axis=0,
        )
        scores = lax.dot_general(
            head_rows, key, (((1,), (1,)), ((), ())), preferred_element_type=f32
        ) * HEAD_DIM ** (-0.5)
        scores = jnp.where(seen, scores.reshape(group, rows, key_count), masked_score)
        top = jnp.max(scores, axis=-1, keepdims=True)
        weights = jnp.where(seen, jnp.exp(scores - top), 0.0)
        denominator = jnp.sum(weights, axis=-1, keepdims=True)
        numerator = jnp.dot(
            weights.astype(bf16).reshape(group * rows, key_count), value, preferred_element_type=f32
        ).reshape(group, rows, HEAD_DIM)
        heads = (numerator / denominator).astype(bf16)
        context[0, h] = jnp.concatenate([heads[g] for g in range(group)], axis=1)
        for s in (2, 1, 3):
            remote(
                context.at[0, h], context.at[s, h], context_send.at[s - 1], context_recv.at[s - 1], ((x + s) % 4, e)
            ).start()

    load.wait()
    depth = group * HEAD_DIM

    def project(s):
        total = None
        for h in range(KV_HEADS):
            term = lax.dot_general(
                context[s, h],
                weight_t[:, pl.ds(h * depth, depth)],
                (((1,), (1,)), ((), ())),
                preferred_element_type=f32,
            )
            total = term if total is None else total + term
        return total.astype(bf16)

    def whole_context(s):
        return remote(
            context.at[0], context.at[s], context_send.at[s - 1], context_recv.at[s - 1], ((x + s) % 4, e)
        )

    columns[x] = project(0)
    all_of(late_out, late_in, late_send, late_recv).wait_recv()
    unpack(late_in)
    for start in range(0, width, PIECE):
        part = min(PIECE, width - start)
        moved = jnp.dot(
            settle, stack[pl.ds(start // PIECE * rows, rows), :], preferred_element_type=f32
        )
        residual[:, pl.ds(start, part)] = moved[:, :part]
    for s in (1, 3, 2):
        whole_context(s).wait_recv()
        parts[s - 1] = project(s)
        remote(parts.at[s - 1], columns.at[x], column_send, column_recv, ((x + 4 - s) % 4, e)).start()
    done = remote(parts, columns.at[pl.ds(0, 3)], column_send, column_recv, ((x + 1) % 4, e))
    done.wait_recv()
    weight_rest()
    update = jnp.concatenate([columns[d] for d in range(4)], axis=1).astype(f32)
    total = residual[...] + update
    residual[...] = total
    scale = lax.rsqrt(jnp.mean(total * total, axis=-1, keepdims=True) + norm_eps)
    normed[...] = (total * scale).astype(bf16)
    done.wait_send()
    keys.wait_send()
    for s in range(1, 4):
        whole_context(s).wait_send()
    all_of(early_out, early_in, early_send, early_recv).wait_send()
    all_of(late_out, late_in, late_send, late_recv).wait_send()


def layer_kernel(
    grid,
    sent,
    destination,
    lengths,
    expert_index,
    router_weights,
    stream_t,
    query,
    key_value,
    weight_hbm,
    own_in,
    own_out,
    result,
    residual,
    normed,
    dispatch,
    combine,
    raw_in,
    split,
    raw_out,
    *rest,
):
    buffers, (weight_sem, out_sem, own_sem, pair_send, pair_recv), sems = rest[:18], rest[18:23], rest[23:]
    cores = grid[0]
    x = lax.axis_index("dp")
    e = lax.axis_index("expert")
    pair = (weight_pair(x, e % cores), e)
    columns = raw_in.shape[1]
    late_rows = pl.ds(sent, columns - sent)

    def to_pair(src, dst, i):
        return pltpu.make_async_remote_copy(
            src_ref=src,
            dst_ref=dst,
            send_sem=pair_send.at[i],
            recv_sem=pair_recv.at[i],
            device_id=pair,
            device_id_type=pl.DeviceIdType.MESH,
        )

    near = to_pair(own_in.at[pl.ds(0, sent)], raw_in.at[1, pl.ds(0, sent)], 0)
    weight_in = to_pair(own_in.at[late_rows], raw_in.at[1, late_rows], 1)
    weight_out = to_pair(own_out, raw_out.at[1], 2)
    load_out = pltpu.make_async_copy(own_out, raw_out.at[0], out_sem)
    load_out.start()

    def weight_rest():
        weight_in.start()
        weight_out.start()

    size = buffers[0].shape[0] * buffers[0].shape[1]
    height, depth = weight_hbm.shape
    if height <= columns and depth <= raw_in.shape[2]:
        weight_t = raw_in.at[0, pl.ds(0, height), pl.ds(0, depth)]
    else:
        weight_t = buffers[17]
    shuffle = [split.at[pl.ds(0, size), pl.ds(i * size, size)] for i in range(2)]
    stack = split.at[pl.ds(0, size), pl.ds(2 * size, PIECE)]
    attention_kernel(
        grid,
        destination,
        lengths,
        expert_index,
        router_weights,
        stream_t,
        query,
        key_value,
        weight_hbm,
        near,
        weight_rest,
        residual,
        normed,
        dispatch,
        combine,
        weight_t,
        shuffle,
        stack,
        *buffers[:9],
        weight_sem,
        *sems[:10],
    )
    expert_kernel(
        grid,
        dispatch,
        normed,
        residual,
        combine,
        near,
        weight_in,
        weight_out,
        load_out,
        own_in,
        result,
        raw_in,
        split,
        raw_out,
        *buffers[9:17],
        own_sem,
        *sems[10:],
    )


def layer(grid, destination, lengths, expert_index, router_weights, stream_t, query, key_value, weight_t, own_in, own_out):
    rows = destination.shape[1]
    width = stream_t.shape[0]
    count = grid[0] * grid[1] * grid[2]
    slab = PIECES * (rows // count)
    slots = rows * TOPK
    capacity = slots // count
    part = slots // 4
    columns = own_in.shape[0]
    units = columns // 2
    padded = -(-units // 128) * 128
    vmem = pl.BlockSpec(memory_space=pltpu.VMEM)
    hbm = pl.BlockSpec(memory_space=pl.ANY)
    dma = pltpu.SemaphoreType.DMA
    slabs = pltpu.VMEM((count, slab, PIECE), bf16)
    buffer = pltpu.VMEM((count, capacity, width), bf16)
    early_width = query.shape[1] + key_value.shape[1]
    carved = weight_t.shape[0] <= columns and weight_t.shape[1] <= width
    return pl.pallas_call(
        functools.partial(layer_kernel, grid, max(columns // 32, 1) * 16),
        out_shape=jax.ShapeDtypeStruct((rows, width), bf16),
        in_specs=[vmem, pl.BlockSpec(memory_space=pltpu.SMEM)] + [vmem] * 5 + [hbm] * 3,
        out_specs=vmem,
        scratch_shapes=[
            pltpu.VMEM((rows, width), f32),
            pltpu.VMEM((rows, width), bf16),
            pltpu.VMEM((slots, rows), bf16),
            pltpu.VMEM((2, rows, slots), bf16),
            pltpu.VMEM((2, columns, width), bf16),
            pltpu.VMEM((4 * padded, width), bf16),
            pltpu.VMEM((2, units, width), bf16),
            slabs,
            slabs,
            slabs,
            slabs,
            pltpu.VMEM((rows, early_width), bf16),
            pltpu.VMEM((4, rows, key_value.shape[1]), bf16),
            pltpu.VMEM((4, KV_HEADS, rows, HEADS // KV_HEADS * HEAD_DIM), bf16),
            pltpu.VMEM((3, rows, width // 4), bf16),
            pltpu.VMEM((4, rows, width // 4), bf16),
            buffer,
            buffer,
            buffer,
            pltpu.VMEM((2 * part, width), bf16),
            pltpu.VMEM((2, 2 * part, padded), bf16),
            pltpu.VMEM((2, part, width), f32),
            buffer,
            buffer,
            pltpu.VMEM((16, 128) if carved else weight_t.shape, bf16),
        ]
        + [dma, dma, dma, dma((3,)), dma((3,))]
        + [dma] * 6
        + [dma((3,))] * 2
        + [dma] * 2
        + [dma((4,))] * 8,
        compiler_params=pltpu.CompilerParams(
            collective_id=2, has_side_effects=True, vmem_limit_bytes=60 << 20
        ),
        cost_estimate=pl.CostEstimate(flops=18 << 30, bytes_accessed=30 << 20, transcendentals=0),
        name="layer",
    )(destination, lengths, expert_index, router_weights, stream_t, query, key_value, weight_t, own_in, own_out)


def on_device(
    stream_rows,
    query_rows,
    key_value_rows,
    destination,
    lengths,
    out_weight,
    expert_index,
    router_weights,
    gate_up,
    down_weight,
):
    row_count, model_width = stream_rows.shape
    expert_count = lax.axis_size("expert")
    cores, ys = 2, 4
    grid = (cores, ys, expert_count // (cores * ys))
    own_in = gate_up[0].T
    scored = layer(
        grid,
        destination.reshape(1, row_count),
        lengths,
        expert_index[0].T,
        router_weights[0].T,
        stream_rows.T,
        query_rows,
        key_value_rows,
        out_weight.T,
        own_in,
        down_weight[0],
    )
    return scored.reshape(1, row_count, model_width)


def solution(mesh):
    placed = (
        P(("dp", "expert"), None),
        P(("dp", "expert"), None),
        P(("dp", "expert"), None),
        P(("dp", "expert")),
        P("expert", None),
        P(None, "dp"),
        P("expert", "dp", None),
        P("expert", "dp", None),
        P("expert", None, "dp"),
        P("expert", "dp", None),
    )
    return jax.shard_map(
        on_device, mesh=mesh, in_specs=placed, out_specs=P("expert", "dp", None), check_vma=False
    )
```

```python
import functools

import jax
import jax.numpy as jnp
from jax import lax
from jax.experimental import pallas as pl
from jax.experimental.pallas import tpu as pltpu
from jax.sharding import PartitionSpec as P

HEADS = 32
KV_HEADS = 4
HEAD_DIM = 64
TOPK = 4


masked_score = -1e30
norm_eps = 1e-05
f32 = jnp.float32
bf16 = jnp.bfloat16


def relation(index, cores, ys, zs):
    per = zs * cores
    half = max(zs // 2, 1)
    chunk, rest = index // per, index % per
    turn = rest // cores
    dz = (turn % 2) * (half + turn // 2) + (1 - turn % 2) * ((half - turn // 2) % half)
    return dz, (chunk + zs * ys - dz) % ys, rest % cores


def peer(expert, index, sign, cores, ys, zs):
    dz, dy, dc = relation(index, cores, ys, zs)
    z, y, c = expert // (ys * cores), (expert // cores) % ys, expert % cores
    z = (z + sign * dz + zs) % zs
    y = (y + sign * dy + ys) % ys
    c = (c + dc) % cores
    return (z * ys + y) * cores + c


def weight_pair(x, core):
    return (x + 5 - 2 * ((x + core) % 2)) % 4


def expert_kernel(
    grid,
    dispatch,
    normed,
    residual,
    combine,
    near,
    weight_in,
    weight_out,
    load_out,
    own_in,
    result,
    raw_in,
    split,
    raw_out,
    out_buf,
    in_own,
    in_twin,
    x_buf,
    h_buf,
    own_part,
    part_recv,
    ret_recv,
    own_sem,
    go_send,
    go_recv,
    twin_send,
    twin_recv,
    part_ssem,
    part_rsem,
    ret_send,
    ret_rsem,
):
    cores, ys, zs = grid
    x = lax.axis_index("dp")
    e = lax.axis_index("expert")
    twin = (weight_pair(x, 1 - e % cores), e)
    slabs, capacity, width = out_buf.shape
    per = slabs // 4
    rows = per * capacity
    columns = raw_in.shape[1]
    units = columns // 2
    padded = split.shape[0] // 4

    def remote(src, dst, ssem, rsem, device):
        return pltpu.make_async_remote_copy(
            src_ref=src, dst_ref=dst, send_sem=ssem, recv_sem=rsem, device_id=device, device_id_type=pl.DeviceIdType.MESH
        )

    load_own = pltpu.make_async_copy(own_in, raw_in.at[0], own_sem)
    load_own.start()

    def chunk_of(ref, c):
        return ref.at[pl.ds(c * per, per)]

    def pack_dispatch(c):
        picked = jnp.dot(dispatch[pl.ds(c * rows, rows), :], normed[...], preferred_element_type=f32)
        out_buf[pl.ds(c * per, per)] = picked.astype(bf16).reshape(per, capacity, width)

    def send_dispatch(c):
        def one(m, carry):
            index = c * per + m
            remote(
                out_buf.at[index], in_own.at[index], go_send.at[c], go_recv.at[c], (x, peer(e, index, 1, cores, ys, zs))
            ).start()
            return carry

        lax.fori_loop(jnp.where(c == 0, 1, 0), per, one, 0)

    def begin(c, carry):
        pack_dispatch(c)
        send_dispatch(c)
        return carry

    lax.fori_loop(0, 4, begin, 0)
    in_own[0] = out_buf[0]

    row = lax.broadcasted_iota(jnp.int32, (2 * padded, columns), 0)
    column = lax.broadcasted_iota(jnp.int32, (2 * padded, columns), 1)
    unit = jnp.where(row < padded, row, row - padded)
    wanted = jnp.where(unit < units, 2 * unit + jnp.where(row < padded, 0, 1), -1)
    part = (column == wanted).astype(f32).astype(bf16)

    def separate(k):
        for start in range(0, width, 768):
            cols = pl.ds(start, min(768, width - start))
            split[pl.ds(k * 2 * padded, 2 * padded), cols] = jnp.dot(part, raw_in[k, :, cols], preferred_element_type=f32).astype(bf16)

    load_own.wait()
    separate(0)
    load_out.wait()
    near.wait()

    def wait_own(c):
        @pl.when(c == 0)
        def _():
            view = in_own.at[pl.ds(1, per - 1)]
            remote(view, view, go_send.at[0], go_recv.at[0], twin).wait_recv()

        @pl.when(c > 0)
        def _():
            view = chunk_of(in_own, c)
            remote(view, view, go_send.at[c], go_recv.at[c], twin).wait_recv()

    def forward(c):
        return remote(chunk_of(in_own, c), chunk_of(in_twin, c), twin_send.at[c], twin_recv.at[c], twin)

    def partial(c):
        return remote(chunk_of(in_twin, c), chunk_of(part_recv, c), part_ssem.at[c], part_rsem.at[c], twin)

    def wait_sent(ref, sems, c):
        @pl.when(c == 0)
        def _():
            view = ref.at[pl.ds(1, per - 1)]
            remote(view, view, sems.at[0], go_recv.at[0], twin).wait_send()

        @pl.when(c > 0)
        def _():
            view = chunk_of(ref, c)
            remote(view, view, sems.at[c], go_recv.at[c], twin).wait_send()

    def compute(c):
        x_buf[pl.ds(0, rows), :] = in_own[pl.ds(c * per, per)].reshape(rows, width)
        x_buf[pl.ds(rows, rows), :] = in_twin[pl.ds(c * per, per)].reshape(rows, width)

        def units_of(k, carry):
            projected = lax.dot_general(
                x_buf[...],
                split[pl.ds(pl.multiple_of(k * 2 * padded, 128), 2 * padded), :],
                (((1,), (1,)), ((), ())), preferred_element_type=f32
            )
            gate = projected[:, :padded]
            up = projected[:, padded:]
            hidden = (up + 1.0) * gate * (1.0 / (1.0 + jnp.exp(-1.702 * gate)))
            h_buf[k] = hidden.astype(bf16)
            return carry

        lax.fori_loop(0, 2, units_of, 0)
        for start in range(0, width, 768):
            size = min(768, width - start)
            cols = pl.ds(start, size)
            total = jnp.dot(h_buf[0, :, :units], raw_out[0, :, cols], preferred_element_type=f32)
            total += jnp.dot(h_buf[1, :, :units], raw_out[1, :, cols], preferred_element_type=f32)
            own_part[c % 2, :, cols] = total[:rows]
            in_twin[pl.ds(c * per, per), :, cols] = total[rows:].astype(bf16).reshape(per, capacity, size)

    def give_back(c):
        wait_sent(out_buf, go_send, c)
        total = own_part[c % 2] + part_recv[pl.ds(c * per, per)].astype(f32).reshape(rows, width)
        out_buf[pl.ds(c * per, per)] = total.astype(bf16).reshape(per, capacity, width)

        def one(m, carry):
            index = c * per + m
            remote(
                out_buf.at[index], ret_recv.at[index], ret_send.at[c], ret_rsem.at[c], (x, peer(e, index, -1, cores, ys, zs))
            ).start()
            return carry

        lax.fori_loop(jnp.where(c == 0, 1, 0), per, one, 0)

    def step(t, carry):
        @pl.when(t < 4)
        def _():
            wait_own(t)
            forward(t).start()

        @pl.when(t == 1)
        def _():
            weight_in.wait()
            separate(1)
            weight_out.wait()

        @pl.when((t >= 1) & (t < 5))
        def _():
            forward(t - 1).wait_recv()
            compute(t - 1)
            partial(t - 1).start()

        @pl.when(t >= 2)
        def _():
            partial(t - 2).wait_recv()
            give_back(t - 2)

        return carry

    lax.fori_loop(0, 6, step, 0)
    ret_recv[0] = out_buf[0]

    for c in range(4):
        view = ret_recv.at[pl.ds(1, per - 1)] if c == 0 else chunk_of(ret_recv, c)
        remote(view, view, go_send.at[0], ret_rsem.at[c], twin).wait_recv()
        for start in range(0, width, 768):
            size = min(768, width - start)
            cols = pl.ds(start, size)
            back = ret_recv[pl.ds(c * per, per), :, cols].reshape(rows, size)
            mixed = residual[:, cols]
            for i in range(2):
                mixed += jnp.dot(combine[i, :, pl.ds(c * rows, rows)], back, preferred_element_type=f32)
            if c < 3:
                residual[:, cols] = mixed
            else:
                result[:, cols] = mixed.astype(bf16)

    def finish(c, carry):
        forward(c).wait_send()
        partial(c).wait_send()
        wait_sent(out_buf, ret_send, c)
        return carry

    lax.fori_loop(0, 4, finish, 0)


PIECE = 384
PIECES = 8


def attention_kernel(
    grid,
    destination,
    lengths,
    expert_index,
    router_weights,
    stream_t,
    query,
    key_value,
    weight_hbm,
    near,
    weight_rest,
    residual,
    normed,
    dispatch,
    combine,
    weight_t,
    shuffle,
    stack,
    early_out,
    early_in,
    late_out,
    late_in,
    sorted_rows,
    section,
    context,
    parts,
    columns,
    local_sem,
    early_send,
    early_recv,
    late_send,
    late_recv,
    key_send,
    key_recv,
    context_send,
    context_recv,
    column_send,
    column_recv,
):
    cores, ys, zs = grid
    x = lax.axis_index("dp")
    e = lax.axis_index("expert")
    count = cores * ys * zs
    rows = destination.shape[1]
    share = rows // count
    width = residual.shape[1]
    slab = PIECES * share
    mesh_id = pl.DeviceIdType.MESH

    def remote(src, dst, ssem, rsem, device):
        return pltpu.make_async_remote_copy(
            src_ref=src, dst_ref=dst, send_sem=ssem, recv_sem=rsem, device_id=device, device_id_type=mesh_id
        )

    barrier = pltpu.get_barrier_semaphore()

    def greet(step, carry):
        pl.semaphore_signal(barrier, inc=1, device_id=(x, (e + step) % count), device_id_type=mesh_id)
        return carry

    lax.fori_loop(1, count, greet, 0)
    for s in range(1, 4):
        pl.semaphore_signal(barrier, inc=1, device_id=((x + s) % 4, e), device_id_type=mesh_id)
    load = pltpu.make_async_copy(weight_hbm, weight_t, local_sem)
    load.start()

    size = count * slab
    row = lax.broadcasted_iota(jnp.int32, (size, 1), 0)
    column = lax.broadcasted_iota(jnp.int32, (size, size), 1)
    source = (row % slab) // share * rows + row // slab * share + row % share
    shuffle[0][...] = (column == source).astype(f32).astype(bf16)

    def pack(values, out):
        stack[...] = jnp.zeros_like(stack)
        for start, value in values:
            done = 0
            while done < value.shape[1]:
                piece, offset = (start + done) // PIECE, (start + done) % PIECE
                part = min(PIECE - offset, value.shape[1] - done)
                stack[pl.ds(piece * rows, rows), pl.ds(offset, part)] = value[:, done : done + part]
                done += part
        out[...] = (
            jnp.dot(shuffle[0][...], stack[...], preferred_element_type=f32).astype(bf16).reshape(count, slab, PIECE)
        )

    def unpack(got):
        stack[...] = jnp.dot(
            shuffle[1][...], got[...].reshape(size, PIECE), preferred_element_type=f32
        ).astype(bf16)

    def send_all(src, dst, ssem, rsem):
        def one(index, carry):
            remote(src.at[index], dst.at[index], ssem, rsem, (x, peer(e, index, 1, cores, ys, zs))).start()
            return carry

        lax.fori_loop(1, count, one, 0)
        dst[0] = src[0]

    def all_of(src, dst, ssem, rsem):
        return remote(src.at[pl.ds(1, count - 1)], dst.at[pl.ds(1, count - 1)], ssem, rsem, (x, (e + 1) % count))

    across = lax.broadcasted_iota(jnp.int32, (rows, rows), 1)
    down = lax.broadcasted_iota(jnp.int32, (rows, rows), 0)
    target_row = jnp.broadcast_to(destination[...], (rows, rows))
    target_col = jnp.sum(jnp.where(across == down, target_row, 0), axis=1, keepdims=True)
    bits = (4 * rows).bit_length() - 1
    pack_row = lax.shift_right_logical(target_row, bits)
    pack_col = lax.shift_right_logical(target_col, bits)
    rank = jnp.sum(((pack_row == pack_col) & (down < across)).astype(jnp.int32), axis=0, keepdims=True)
    index = lax.broadcasted_iota(jnp.int32, (rows, 1), 0)
    slot = peer(e, index // share, 1, cores, ys, zs) * share + index % share
    sender = (slot == pack_row * share + rank).astype(f32).astype(bf16)
    lane = lax.broadcasted_iota(jnp.int32, (rows, 128), 1)
    place = (lane == (target_col & (rows - 1))).astype(f32).astype(bf16)

    query_width, memory_width = query.shape[1], key_value.shape[1]
    early_width = query_width + memory_width
    pack(
        [
            (0, jnp.dot(sender, query[...], preferred_element_type=f32).astype(bf16)),
            (query_width, jnp.dot(sender, key_value[...], preferred_element_type=f32).astype(bf16)),
            (early_width, jnp.dot(sender, place, preferred_element_type=f32).astype(bf16)),
        ],
        early_out,
    )
    pl.semaphore_wait(barrier, count + 2)
    near.start()
    send_all(early_out, early_in, early_send, early_recv)
    pack(
        [
            (
                0,
                lax.dot_general(
                    sender, stream_t[...], (((1,), (1,)), ((), ())), preferred_element_type=f32
                ).astype(bf16),
            )
        ],
        late_out,
    )
    send_all(late_out, late_in, late_send, late_recv)
    source = (row % rows) // share * slab + row // rows * share + row % share
    shuffle[1][...] = (column == source).astype(f32).astype(bf16)

    slots, capacity = dispatch.shape[0], dispatch.shape[0] // count
    holder = peer(e, lax.broadcasted_iota(jnp.int32, (count, 1), 0), 1, cores, ys, zs)
    chosen = jnp.zeros((count, rows), f32)
    weight = jnp.zeros((count, rows), f32)
    for k in range(TOPK):
        match = holder == expert_index[k : k + 1, :]
        chosen += match.astype(f32)
        weight += jnp.where(match, router_weights[k : k + 1, :], 0.0)
    before = (down < across).astype(f32).astype(bf16)
    earlier = jnp.dot(chosen.astype(bf16), before, preferred_element_type=f32)
    earlier = jnp.where(chosen > 0.0, earlier, -1.0)
    slot_row = lax.broadcasted_iota(jnp.int32, (slots, count), 0)
    spread = (slot_row // capacity == lax.broadcasted_iota(jnp.int32, (slots, count), 1)).astype(f32).astype(bf16)
    number = (lax.broadcasted_iota(jnp.int32, (slots, rows), 0) % capacity).astype(f32)
    taken = jnp.dot(spread, earlier.astype(bf16), preferred_element_type=f32) == number
    dispatch[...] = taken.astype(f32).astype(bf16)
    high = weight.astype(bf16)
    low = (weight - high.astype(f32)).astype(bf16)
    for i, value in enumerate((high, low)):
        wide = jnp.dot(spread, value, preferred_element_type=f32)
        combine[i] = jnp.transpose(jnp.where(taken, wide, 0.0)).astype(bf16)

    all_of(early_out, early_in, early_send, early_recv).wait_recv()
    unpack(early_in)
    last, offset = early_width // PIECE, early_width % PIECE
    spots = stack[pl.ds(last * rows, rows), pl.ds(offset, 128)].astype(f32)
    settle = jnp.transpose(spots)[:rows].astype(bf16)

    def move_piece(piece):
        part = min(PIECE, early_width - piece * PIECE)
        moved = jnp.dot(settle, stack[pl.ds(piece * rows, rows), :], preferred_element_type=f32).astype(bf16)
        sorted_rows[:, pl.ds(piece * PIECE, part)] = moved[:, :part]

    for piece in range(query_width // PIECE, last + 1):
        move_piece(piece)
    section[0] = sorted_rows[:, pl.ds(query_width, memory_width)]
    for s in range(1, 4):
        remote(section.at[0], section.at[s], key_send, key_recv, ((x + s) % 4, e)).start()
    for piece in range(query_width // PIECE):
        move_piece(piece)

    keys = remote(section.at[pl.ds(1, 3)], section.at[pl.ds(1, 3)], key_send, key_recv, ((x + 1) % 4, e))
    keys.wait_recv()
    key_count = 4 * rows
    group = HEADS // KV_HEADS
    key_width = KV_HEADS * HEAD_DIM
    first, second = lengths[0, 0], lengths[0, 0] + lengths[0, 1]

    def segment(position):
        return (position >= first).astype(jnp.int32) + (position >= second).astype(jnp.int32)

    key_lane = lax.broadcasted_iota(jnp.int32, (rows, key_count), 1)
    key_place = (x + 4 - key_lane // rows) % 4 * rows + key_lane % rows
    query_place = x * rows + lax.broadcasted_iota(jnp.int32, (rows, key_count), 0)
    seen = ((segment(key_place) == segment(query_place)) & (key_place <= query_place))[None]
    def context_piece(s, h):
        near_by = s != 2
        source = 0 if near_by else 1 + 2 * (h % 2)
        step = s if near_by else source
        return remote(
            context.at[source, h],
            context.at[s, h],
            context_send.at[(s - 1) * KV_HEADS + h],
            context_recv.at[(s - 1) * KV_HEADS + h],
            ((x + step) % 4, e),
        )

    def pass_on(h):
        context_piece(1 + 2 * (h % 2), h).wait_recv()
        context_piece(2, h).start()

    for h in range(KV_HEADS):
        key = section[:, :, h * HEAD_DIM : (h + 1) * HEAD_DIM].reshape(key_count, HEAD_DIM)
        value = section[:, :, key_width + h * HEAD_DIM : key_width + (h + 1) * HEAD_DIM].reshape(
            key_count, HEAD_DIM
        )
        head_rows = jnp.concatenate(
            [
                sorted_rows[:, (h * group + g) * HEAD_DIM : (h * group + g + 1) * HEAD_DIM]
                for g in range(group)
            ],
            axis=0,
        )
        scores = lax.dot_general(
            head_rows, key, (((1,), (1,)), ((), ())), preferred_element_type=f32
        ) * HEAD_DIM ** (-0.5)
        scores = jnp.where(seen, scores.reshape(group, rows, key_count), masked_score)
        top = jnp.max(scores, axis=-1, keepdims=True)
        weights = jnp.where(seen, jnp.exp(scores - top), 0.0)
        denominator = jnp.sum(weights, axis=-1, keepdims=True)
        numerator = jnp.dot(
            weights.astype(bf16).reshape(group * rows, key_count), value, preferred_element_type=f32
        ).reshape(group, rows, HEAD_DIM)
        heads = (numerator / denominator).astype(bf16)
        context[0, h] = jnp.concatenate([heads[g] for g in range(group)], axis=1)
        for s in (1, 3):
            context_piece(s, h).start()
        if h >= 2:
            pass_on(h - 2)

    for h in range(KV_HEADS - 2, KV_HEADS):
        pass_on(h)
    load.wait()
    depth = group * HEAD_DIM

    def project(s):
        total = None
        for h in range(KV_HEADS):
            term = lax.dot_general(
                context[s, h],
                weight_t[:, pl.ds(h * depth, depth)],
                (((1,), (1,)), ((), ())),
                preferred_element_type=f32,
            )
            total = term if total is None else total + term
        return total.astype(bf16)

    columns[x] = project(0)
    all_of(late_out, late_in, late_send, late_recv).wait_recv()
    unpack(late_in)
    for start in range(0, width, PIECE):
        part = min(PIECE, width - start)
        moved = jnp.dot(
            settle, stack[pl.ds(start // PIECE * rows, rows), :], preferred_element_type=f32
        )
        residual[:, pl.ds(start, part)] = moved[:, :part]
    for s in (1, 3, 2):
        for h in range(KV_HEADS):
            if s != 1 + 2 * (h % 2):
                context_piece(s, h).wait_recv()
        parts[s - 1] = project(s)
        remote(parts.at[s - 1], columns.at[x], column_send, column_recv, ((x + 4 - s) % 4, e)).start()
    done = remote(parts, columns.at[pl.ds(0, 3)], column_send, column_recv, ((x + 1) % 4, e))
    done.wait_recv()
    weight_rest()
    update = jnp.concatenate([columns[d] for d in range(4)], axis=1).astype(f32)
    total = residual[...] + update
    residual[...] = total
    scale = lax.rsqrt(jnp.mean(total * total, axis=-1, keepdims=True) + norm_eps)
    normed[...] = (total * scale).astype(bf16)
    done.wait_send()
    keys.wait_send()
    for s in range(1, 4):
        for h in range(KV_HEADS):
            context_piece(s, h).wait_send()
    all_of(early_out, early_in, early_send, early_recv).wait_send()
    all_of(late_out, late_in, late_send, late_recv).wait_send()


def layer_kernel(
    grid,
    sent,
    destination,
    lengths,
    expert_index,
    router_weights,
    stream_t,
    query,
    key_value,
    weight_hbm,
    own_in,
    own_out,
    result,
    residual,
    normed,
    dispatch,
    combine,
    raw_in,
    split,
    raw_out,
    *rest,
):
    buffers, (weight_sem, out_sem, own_sem, pair_send, pair_recv), sems = rest[:18], rest[18:23], rest[23:]
    cores = grid[0]
    x = lax.axis_index("dp")
    e = lax.axis_index("expert")
    pair = (weight_pair(x, e % cores), e)
    columns = raw_in.shape[1]
    late_rows = pl.ds(sent, columns - sent)

    def to_pair(src, dst, i):
        return pltpu.make_async_remote_copy(
            src_ref=src,
            dst_ref=dst,
            send_sem=pair_send.at[i],
            recv_sem=pair_recv.at[i],
            device_id=pair,
            device_id_type=pl.DeviceIdType.MESH,
        )

    near = to_pair(own_in.at[pl.ds(0, sent)], raw_in.at[1, pl.ds(0, sent)], 0)
    weight_in = to_pair(own_in.at[late_rows], raw_in.at[1, late_rows], 1)
    weight_out = to_pair(own_out, raw_out.at[1], 2)
    load_out = pltpu.make_async_copy(own_out, raw_out.at[0], out_sem)
    load_out.start()

    def weight_rest():
        weight_in.start()
        weight_out.start()

    size = buffers[0].shape[0] * buffers[0].shape[1]
    height, depth = weight_hbm.shape
    if height <= columns and depth <= raw_in.shape[2]:
        weight_t = raw_in.at[0, pl.ds(0, height), pl.ds(0, depth)]
    else:
        weight_t = buffers[17]
    shuffle = [split.at[pl.ds(0, size), pl.ds(i * size, size)] for i in range(2)]
    stack = split.at[pl.ds(0, size), pl.ds(2 * size, PIECE)]
    attention_kernel(
        grid,
        destination,
        lengths,
        expert_index,
        router_weights,
        stream_t,
        query,
        key_value,
        weight_hbm,
        near,
        weight_rest,
        residual,
        normed,
        dispatch,
        combine,
        weight_t,
        shuffle,
        stack,
        *buffers[:9],
        weight_sem,
        *sems[:10],
    )
    expert_kernel(
        grid,
        dispatch,
        normed,
        residual,
        combine,
        near,
        weight_in,
        weight_out,
        load_out,
        own_in,
        result,
        raw_in,
        split,
        raw_out,
        *buffers[9:17],
        own_sem,
        *sems[10:],
    )


def layer(grid, destination, lengths, expert_index, router_weights, stream_t, query, key_value, weight_t, own_in, own_out):
    rows = destination.shape[1]
    width = stream_t.shape[0]
    count = grid[0] * grid[1] * grid[2]
    slab = PIECES * (rows // count)
    slots = rows * TOPK
    capacity = slots // count
    part = slots // 4
    columns = own_in.shape[0]
    units = columns // 2
    padded = -(-units // 128) * 128
    vmem = pl.BlockSpec(memory_space=pltpu.VMEM)
    hbm = pl.BlockSpec(memory_space=pl.ANY)
    dma = pltpu.SemaphoreType.DMA
    slabs = pltpu.VMEM((count, slab, PIECE), bf16)
    buffer = pltpu.VMEM((count, capacity, width), bf16)
    early_width = query.shape[1] + key_value.shape[1]
    carved = weight_t.shape[0] <= columns and weight_t.shape[1] <= width
    return pl.pallas_call(
        functools.partial(layer_kernel, grid, max(columns // 32, 1) * 16),
        out_shape=jax.ShapeDtypeStruct((rows, width), bf16),
        in_specs=[vmem, pl.BlockSpec(memory_space=pltpu.SMEM)] + [vmem] * 5 + [hbm] * 3,
        out_specs=vmem,
        scratch_shapes=[
            pltpu.VMEM((rows, width), f32),
            pltpu.VMEM((rows, width), bf16),
            pltpu.VMEM((slots, rows), bf16),
            pltpu.VMEM((2, rows, slots), bf16),
            pltpu.VMEM((2, columns, width), bf16),
            pltpu.VMEM((4 * padded, width), bf16),
            pltpu.VMEM((2, units, width), bf16),
            slabs,
            slabs,
            slabs,
            slabs,
            pltpu.VMEM((rows, early_width), bf16),
            pltpu.VMEM((4, rows, key_value.shape[1]), bf16),
            pltpu.VMEM((4, KV_HEADS, rows, HEADS // KV_HEADS * HEAD_DIM), bf16),
            pltpu.VMEM((3, rows, width // 4), bf16),
            pltpu.VMEM((4, rows, width // 4), bf16),
            buffer,
            buffer,
            buffer,
            pltpu.VMEM((2 * part, width), bf16),
            pltpu.VMEM((2, 2 * part, padded), bf16),
            pltpu.VMEM((2, part, width), f32),
            buffer,
            buffer,
            pltpu.VMEM((16, 128) if carved else weight_t.shape, bf16),
        ]
        + [dma, dma, dma, dma((3,)), dma((3,))]
        + [dma] * 6
        + [dma((3 * KV_HEADS,))] * 2
        + [dma] * 2
        + [dma((4,))] * 8,
        compiler_params=pltpu.CompilerParams(
            collective_id=2, has_side_effects=True, vmem_limit_bytes=60 << 20
        ),
        cost_estimate=pl.CostEstimate(flops=18 << 30, bytes_accessed=30 << 20, transcendentals=0),
        name="layer",
    )(destination, lengths, expert_index, router_weights, stream_t, query, key_value, weight_t, own_in, own_out)


def on_device(
    stream_rows,
    query_rows,
    key_value_rows,
    destination,
    lengths,
    out_weight,
    expert_index,
    router_weights,
    gate_up,
    down_weight,
):
    row_count, model_width = stream_rows.shape
    expert_count = lax.axis_size("expert")
    cores, ys = 2, 4
    grid = (cores, ys, expert_count // (cores * ys))
    own_in = gate_up[0].T
    scored = layer(
        grid,
        destination.reshape(1, row_count),
        lengths,
        expert_index[0].T,
        router_weights[0].T,
        stream_rows.T,
        query_rows,
        key_value_rows,
        out_weight.T,
        own_in,
        down_weight[0],
    )
    return scored.reshape(1, row_count, model_width)


def solution(mesh):
    placed = (
        P(("dp", "expert"), None),
        P(("dp", "expert"), None),
        P(("dp", "expert"), None),
        P(("dp", "expert")),
        P("expert", None),
        P(None, "dp"),
        P("expert", "dp", None),
        P("expert", "dp", None),
        P("expert", None, "dp"),
        P("expert", "dp", None),
    )
    return jax.shard_map(
        on_device, mesh=mesh, in_specs=placed, out_specs=P("expert", "dp", None), check_vma=False
    )
```
